128 devices in a mesh: gz: 32 (over x, y, core), gy: 4 (over z).
Axes of the slice: x: 4, y: 4, z: 4, core: 2. Of those that a mesh axis runs over, the one named last changes fastest.
Arguments:
- distribution_functions: float32 [19, 128, 36864], P(None, 'gz', 'gy')
- site_phase_kinds: int32 [128, 36864], P('gz', 'gy'), may hold values from 0 to 2
- thermal_state_values: float32 [128, 36864], P('gz', 'gy'), may hold values from 0.5 to 3
- boundary_tile_lines: int32 [128, 64], P(('gz', 'gy')), may hold values from 0 to 287
- wanted_tile_position: int32 [128, 128, 4], P(('gz', 'gy')), may hold values from 0 to 63
- trajectory_hit_places: int32 [128, 512], P(('gz', 'gy')), may hold values from 0 to 511, each once within a row
- hits_along_each_shot: int32 [128, 64], P(('gz', 'gy')), may hold values from 1 to 8
- incident_light_strength: float32 [128, 64, 128], P(('gz', 'gy')), may hold values from 0.5 to 2
Outputs:
- lattice_out: float32 [19, 128, 36864], P(None, 'gz', 'gy')
- temperature_out: float32 [128, 36864], P('gz', 'gy')
The draws below stay inside these ranges and needn't reach their ends.
Inputs may be any that keep to these rules, and one draw needn't show every extreme that they name: `trajectory_hit_places`: each device's row lists every slot exactly once.
All inputs are finite; a program needn't handle non-finite values.
Results may differ from the reference program's by a relative error of at most 0.0003.
Values sent between devices are 32-bit elements; how exact they have to be, the bound alone decides.
A program may use at most 320 MiB of HBM per device.

```python
import math
import jax
import jax.numpy as jnp
import numpy as np
from jax import lax

SITES_ACROSS = 192
CY = 48
CZ = 4
BLOCK = 128
NB_DEV = 64
CAP = 4
BOUNCES = 8
SITES_LENGTHWISE = 192
SITES_VERTICAL = 128
RAY_DEV = 64
N_GZ = 32
N_GY = 4
DEVICES = 128


lattice_wts = [1.0 / 3.0] + [1.0 / 18.0] * 6 + [1.0 / 36.0] * 12


def draw_distribution_functions(key, part):
    spread = 0.25
    noise = jax.random.uniform(key, (19, SITES_VERTICAL, SITES_LENGTHWISE * SITES_ACROSS), jnp.float32, -1.0, 1.0)
    weights = jnp.asarray(np.array(lattice_wts, np.float32))[:, None, None]
    return weights * (1.0 + spread * noise)


def with_ends(values, rng, smallest, high):
    index_at = [jax.random.randint(jax.random.fold_in(rng, axis), (), 0, length) for axis, length in enumerate(values.shape)]
    longest = values.shape.index(max(values.shape))
    next_to = index_at[:longest] + [(index_at[longest] + 1) % values.shape[longest]] + index_at[longest + 1:]
    return values.at[tuple(index_at)].set(smallest).at[tuple(next_to)].set(high)


def levels(own_key, dims, pieces, least, high):
    loudness, own = 1.0, jax.random.fold_in(own_key, 6)
    for dim, shards_of in pieces:
        heights = jnp.exp(jax.random.uniform(jax.random.fold_in(own, dim), (shards_of,), jnp.float32, least / len(pieces), high / len(pieces)))
        loudness = loudness * jnp.repeat(heights, dims[dim] // shards_of).reshape([-1 if axis == dim else 1 for axis in range(len(dims))])
    return loudness


def setup_inputs(seed: int = 0) -> dict:
    key_of = jax.random.split(jax.random.key(seed), 9)
    distribution_functions = draw_distribution_functions(jax.random.fold_in(key_of[8], 71), 0)
    site_phase_kinds = with_ends(jax.random.randint(key_of[1], (SITES_VERTICAL, SITES_LENGTHWISE * SITES_ACROSS), 0, 3), jax.random.fold_in(key_of[1], 1), 0, 2).astype(jnp.int32)
    thermal_state_values = jnp.clip(0.5 + 2.5 * jax.random.uniform(key_of[2], (SITES_VERTICAL, SITES_LENGTHWISE * SITES_ACROSS), jnp.float32) ** levels(key_of[2], (SITES_VERTICAL, SITES_LENGTHWISE * SITES_ACROSS), ((0, 32), (1, 4)), -0.2, 0.2), 0.5, 3.0)
    boundary_tile_lines = with_ends(jax.random.randint(key_of[3], (DEVICES, NB_DEV), 0, CZ * CY * SITES_ACROSS // BLOCK), jax.random.fold_in(key_of[3], 1), 0, (CZ * CY * SITES_ACROSS // BLOCK) - 1).astype(jnp.int32)
    wanted_tile_position = with_ends(jax.random.randint(key_of[4], (DEVICES, DEVICES, CAP), 0, NB_DEV), jax.random.fold_in(key_of[4], 1), 0, NB_DEV - 1).astype(jnp.int32)
    trajectory_hit_places = jax.vmap(lambda own: jax.random.permutation(own, DEVICES * CAP))(jax.random.split(key_of[5], DEVICES)).reshape((DEVICES, DEVICES * CAP)).astype(jnp.int32)
    hits_along_each_shot = with_ends(jax.random.randint(key_of[6], (DEVICES, RAY_DEV), 1, BOUNCES + 1), jax.random.fold_in(key_of[6], 1), 1, BOUNCES).astype(jnp.int32)
    incident_light_strength = jnp.clip(jnp.exp(math.log(2.0) - 1.3862944 * jax.random.uniform(key_of[7], (DEVICES, RAY_DEV, BLOCK), jnp.float32) ** levels(key_of[7], (DEVICES, RAY_DEV, BLOCK), ((0, 128),), -0.2, 0.2)), 0.5, 2.0)
    return {"distribution_functions": distribution_functions, "site_phase_kinds": site_phase_kinds, "thermal_state_values": thermal_state_values, "boundary_tile_lines": boundary_tile_lines, "wanted_tile_position": wanted_tile_position, "trajectory_hit_places": trajectory_hit_places, "hits_along_each_shot": hits_along_each_shot, "incident_light_strength": incident_light_strength}


lattice_dirs = [(0, 0, 0), (1, 0, 0), (-1, 0, 0), (0, 1, 0), (0, -1, 0), (0, 0, 1), (0, 0, -1), (1, 1, 0), (-1, -1, 0), (1, -1, 0), (-1, 1, 0), (1, 0, 1), (-1, 0, -1), (1, 0, -1), (-1, 0, 1), (0, 1, 1), (0, -1, -1), (0, 1, -1), (0, -1, 1)]
reverse_dir = [0, 2, 1, 4, 3, 6, 5, 8, 7, 10, 9, 12, 11, 14, 13, 16, 15, 18, 17]
lattice_wts = [1.0 / 3.0] + [1.0 / 18.0] * 6 + [1.0 / 36.0] * 12
relax_rate = 0.8
taken_power_share = 1.0
thermal_dirs = [(0, 0, 0), (1, 0, 0), (-1, 0, 0), (0, 1, 0), (0, -1, 0), (0, 0, 1), (0, 0, -1)]
thermal_wts = [0.25] + [0.125] * 6


def moments(grid_quantities):
    table = jnp.asarray(np.array(lattice_dirs, np.float32), dtype=grid_quantities.dtype)
    density = jnp.sum(grid_quantities, axis=0)
    momentum = jnp.einsum("qa,qzyx->azyx", table, grid_quantities, precision=lax.Precision.HIGHEST)
    return density, momentum / density[None]


def equilibrium(density, liquid_flow_speed):
    table = jnp.asarray(np.array(lattice_dirs, np.float32), dtype=liquid_flow_speed.dtype)
    project = jnp.einsum("qa,azyx->qzyx", table, liquid_flow_speed, precision=lax.Precision.HIGHEST)
    speed = jnp.sum(liquid_flow_speed * liquid_flow_speed, axis=0)
    weights = jnp.asarray(np.array(lattice_wts, np.float32), dtype=liquid_flow_speed.dtype)[:, None, None, None]
    return weights * density[None] * (1.0 + 3.0 * project + 4.5 * project * project - 1.5 * speed[None])


def lattice_step(padded, gas_pad):
    density, liquid_flow_speed = moments(padded)
    relaxed = padded + relax_rate * (equilibrium(density, liquid_flow_speed) - padded)
    relaxed = jnp.where(gas_pad[None], padded, relaxed)
    depth = padded.shape[1] - 2
    width = padded.shape[2] - 2
    free_eq = equilibrium(jnp.ones_like(density[1:-1, 1:-1]), liquid_flow_speed[:, 1:-1, 1:-1])
    centre_post = relaxed[:, 1:-1, 1:-1]
    moved = []
    for number in range(19):
        step_x, step_y, step_z = lattice_dirs[number]
        thermal_power_term = relaxed[number, 1 - step_z:1 - step_z + depth, 1 - step_y:1 - step_y + width, :]
        thermal_power_term = jnp.roll(thermal_power_term, step_x, axis=-1)
        empty = gas_pad[1 - step_z:1 - step_z + depth, 1 - step_y:1 - step_y + width, :]
        empty = jnp.roll(empty, step_x, axis=-1)
        back = reverse_dir[number]
        rebuilt = free_eq[number] + free_eq[back] - centre_post[back]
        moved.append(jnp.where(empty, rebuilt, thermal_power_term))
    passed = jnp.stack(moved)
    return jnp.where(gas_pad[None, 1:-1, 1:-1], padded[:, 1:-1, 1:-1], passed)


def boundary_mirror_factor(grid_quantities, thermal_state_values, vapour_site_indicator):
    density, liquid_flow_speed = moments(grid_quantities)
    cosine = 0.2 + 0.7 * jax.nn.sigmoid(8.0 * (density - 1.0))
    site_position = 1.0 + thermal_state_values
    upper = (site_position - cosine) * (site_position - cosine) + 1.0
    lower = (site_position + cosine) * (site_position + cosine) + 1.0
    return jnp.where(vapour_site_indicator, jnp.ones_like(upper), upper / lower), liquid_flow_speed


def thermal_terms(thermal_power_term, liquid_flow_speed):
    terms = []
    for number in range(7):
        step_x, step_y, step_z = thermal_dirs[number]
        along = step_x * liquid_flow_speed[0] + step_y * liquid_flow_speed[1] + step_z * liquid_flow_speed[2]
        terms.append(thermal_wts[number] * thermal_power_term * (1.0 + 4.0 * along))
    return terms


def owner_heat(slot_reflect, slots, bounces, beam):
    rays = slot_reflect[slots].reshape(-1, BOUNCES, BLOCK)
    energy = beam
    parts = []
    for bounce in range(BOUNCES):
        ratio = rays[:, bounce]
        live = (bounce < bounces).astype(beam.dtype)[:, None]
        parts.append(energy * (1.0 - ratio) * live)
        energy = energy * ratio
    heat = jnp.stack(parts, axis=1).reshape(-1, BLOCK)
    return jnp.zeros_like(slot_reflect).at[slots].set(heat)


def reference(distribution_functions, site_phase_kinds, thermal_state_values, boundary_tile_lines, wanted_tile_position, trajectory_hit_places, hits_along_each_shot, incident_light_strength):
    distribution_functions = distribution_functions.reshape(19, SITES_VERTICAL, SITES_LENGTHWISE, SITES_ACROSS)
    site_phase_kinds = site_phase_kinds.reshape(SITES_VERTICAL, SITES_LENGTHWISE, SITES_ACROSS)
    thermal_state_values = thermal_state_values.reshape(SITES_VERTICAL, SITES_LENGTHWISE, SITES_ACROSS)
    vapour_share = site_phase_kinds == 0
    grid_quantities = distribution_functions
    for sweep in range(2):
        padded = jnp.pad(grid_quantities, ((0, 0), (1, 1), (1, 1), (0, 0)), mode="wrap")
        gas_pad = jnp.pad(vapour_share, ((1, 1), (1, 1), (0, 0)), mode="wrap")
        grid_quantities = lattice_step(padded, gas_pad)
    mirror_light_shot, liquid_flow_speed = boundary_mirror_factor(grid_quantities, thermal_state_values, vapour_share)
    rows = CZ * CY * SITES_ACROSS // BLOCK
    cells = mirror_light_shot.reshape(N_GZ, CZ, N_GY, CY, SITES_ACROSS).transpose(0, 2, 1, 3, 4).reshape(DEVICES, rows, BLOCK)
    table = jax.vmap(lambda held, picks: held[picks])(cells, boundary_tile_lines)
    slot_reflect = jax.vmap(lambda asked: jax.vmap(lambda held, picks: held[picks])(table, asked))(wanted_tile_position)
    slot_reflect = slot_reflect.reshape(DEVICES, DEVICES * CAP, BLOCK)
    heat = jax.vmap(owner_heat)(slot_reflect, trajectory_hit_places, hits_along_each_shot, incident_light_strength).reshape(DEVICES, DEVICES, CAP, BLOCK)

    def collect(asked, values):
        return jnp.zeros((NB_DEV, BLOCK), values.dtype).at[asked.reshape(-1)].add(values.reshape(-1, BLOCK))

    block_heat = jax.vmap(collect, in_axes=(1, 1))(wanted_tile_position, heat)

    def spread(picks, values):
        return jnp.zeros((rows, BLOCK), values.dtype).at[picks].add(values)

    cell_heat = jax.vmap(spread)(boundary_tile_lines, block_heat)
    place_power_onto_sites = cell_heat.reshape(N_GZ, N_GY, CZ, CY, SITES_ACROSS).transpose(0, 2, 1, 3, 4).reshape(SITES_VERTICAL, SITES_LENGTHWISE, SITES_ACROSS)
    thermal_power_term = thermal_state_values + taken_power_share * place_power_onto_sites
    terms = thermal_terms(thermal_power_term, liquid_flow_speed)
    result = jnp.zeros_like(thermal_power_term)
    for number in range(7):
        step_x, step_y, step_z = thermal_dirs[number]
        result = result + jnp.roll(terms[number], (step_z, step_y, step_x), axis=(0, 1, 2))
    return grid_quantities.reshape(19, SITES_VERTICAL, SITES_LENGTHWISE * SITES_ACROSS), result.reshape(SITES_VERTICAL, SITES_LENGTHWISE * SITES_ACROSS)
```

```python
import jax
import jax.numpy as jnp
from jax import lax
from jax.experimental import pallas as pl
from jax.experimental.pallas import tpu as pltpu
from jax.sharding import PartitionSpec as P

MESH = pl.DeviceIdType.MESH
N_GZ = 32
N_GY = 4
DEVICES = 128
CAP = 4
SLOTS = 512
NB_DEV = 64
RAYS = 64
BOUNCES = 8
ACROSS = 192
DEPTH = 4
ROWS = 72
CELL_ROWS = 288
PAD = 8
PLANE = ROWS + 2 * PAD

DIRS = [
    (0, 0, 0),
    (1, 0, 0),
    (-1, 0, 0),
    (0, 1, 0),
    (0, -1, 0),
    (0, 0, 1),
    (0, 0, -1),
    (1, 1, 0),
    (-1, -1, 0),
    (1, -1, 0),
    (-1, 1, 0),
    (1, 0, 1),
    (-1, 0, -1),
    (1, 0, -1),
    (-1, 0, 1),
    (0, 1, 1),
    (0, -1, -1),
    (0, 1, -1),
    (0, -1, 1),
]
WEIGHTS = [1.0 / 3.0] + [1.0 / 18.0] * 6 + [1.0 / 36.0] * 12
PAIRS = [(q, q + 1) for q in range(1, 19, 2)]
OPP = [0, 2, 1, 4, 3, 6, 5, 8, 7, 10, 9, 12, 11, 14, 13, 16, 15, 18, 17]
RELAX = 0.8
ORDER = [18, 5, 11, 14, 15, 17, 12, 13, 6, 16, 4, 8, 9, 1, 2, 0, 3, 7, 10]
SLOT = [ORDER.index(q) for q in range(19)]
LEFT_BIT = 19
RIGHT_BIT = 20


def tile_iota(axis, shape=(8, 128)):
    return lax.broadcasted_iota(jnp.int32, shape, axis)


def moments(f):
    d = {a: f[a] - f[b] for a, b in PAIRS}
    s = {a: f[a] + f[b] for a, b in PAIRS}
    density = (
        ((s[1] + s[3]) + (s[5] + s[7])) + ((s[9] + s[11]) + (s[13] + s[15])) + (s[17] + f[0])
    )
    mx = (d[1] + d[7]) + (d[9] + d[11]) + d[13]
    my = (d[3] + d[7]) + (d[15] - d[9]) + d[17]
    mz = (d[5] + d[11]) + (d[15] - d[13]) - d[17]
    inv = 1.0 / density
    return density, mx * inv, my * inv, mz * inv


def along(u, q):
    total = None
    for step, part in zip(DIRS[q], u):
        if step == 0:
            continue
        if total is None:
            total = part if step > 0 else -part
        else:
            total = total + part if step > 0 else total - part
    return total


def collide(f, gas):
    density, ux, uy, uz = moments(f)
    base = 1.0 - 1.5 * (ux * ux + uy * uy + uz * uz)
    triple = (3.0 * ux, 3.0 * uy, 3.0 * uz)
    kept = [None] * 19
    keep = 1.0 - RELAX
    scaled = {w: (RELAX * w) * density for w in (1.0 / 18.0, 1.0 / 36.0)}
    post = keep * f[0] + (RELAX / 3.0) * density * base
    kept[0] = jnp.where(gas, -f[0], post)
    for a, b in PAIRS:
        wd = scaled[WEIGHTS[a]]
        c = along(triple, a)
        even = wd * (base + 0.5 * (c * c))
        odd = wd * c
        kept[a] = jnp.where(gas, -f[b], keep * f[a] + (even + odd))
        kept[b] = jnp.where(gas, -f[a], keep * f[b] + (even - odd))
    zero = jnp.zeros_like(ux)
    velocity = [jnp.where(gas, zero, v) for v in (ux, uy, uz, base)]
    return kept, velocity


def shifted(load, step_x, step_y, left, right):
    lane = tile_iota(1)

    def flat(by):
        rows, lanes = by // 128, by % 128
        if lanes == 0:
            return load(-rows)
        picked = jnp.where(lane >= 128 - lanes, load(-rows - 1), load(-rows))
        return pltpu.roll(picked, lanes, 1)

    main = flat(step_x + ACROSS * step_y)
    if step_x == 0:
        return main
    by = step_x + ACROSS * step_y - ACROSS * step_x
    rows, lanes = by // 128, by % 128
    targets = (0, 64) if step_x == 1 else (63, 127)
    if all(t < lanes for t in targets):
        wrapped = pltpu.roll(load(-rows - 1), lanes, 1)
    elif all(t >= lanes for t in targets):
        wrapped = pltpu.roll(load(-rows), lanes, 1)
    else:
        wrapped = flat(by)
    return jnp.where(left if step_x == 1 else right, wrapped, main)


def window(ref, lead, z, rb):
    def load(n):
        return ref[(*lead, z, pl.ds(rb * 8 + (PAD + n), 8), slice(None))]

    return load


def passed(post_ref, mask_ref, vel_ref, z, rb):
    mask = mask_ref[z, pl.ds(rb * 8, 8), :]
    left = (mask & (1 << LEFT_BIT)) != 0
    right = (mask & (1 << RIGHT_BIT)) != 0
    ux, uy, uz, base = [vel_ref[i, z, pl.ds(rb * 8, 8), :] for i in range(4)]
    centre = [post_ref[SLOT[q], z + 1, pl.ds(rb * 8 + PAD, 8), :] for q in range(19)]
    new = [None] * 19
    new[0] = jnp.where((mask & 1) != 0, -centre[0], centre[0])
    triple = (3.0 * ux, 3.0 * uy, 3.0 * uz)
    for a, b in PAIRS:
        c = along(triple, a)
        both = (2.0 * WEIGHTS[a]) * (base + 0.5 * (c * c))
        for q, back in ((a, b), (b, a)):
            step_x, step_y, step_z = DIRS[q]
            source = shifted(
                window(post_ref, (SLOT[q],), z + 1 - step_z, rb), step_x, step_y, left, right
            )
            new[q] = jnp.where((mask & (1 << q)) != 0, both - centre[back], source)
    return new, (mask & 1) != 0


def two_terms(x):
    high = x.astype(jnp.bfloat16)
    low = (x - high.astype(jnp.float32)).astype(jnp.bfloat16)
    return jnp.concatenate([high, low], axis=1)


def pick(one_hot, values):
    both = jnp.dot(one_hot, two_terms(values), preferred_element_type=jnp.float32)
    return both[:, :128] + both[:, 128:]


def edge_tile(j):
    late = lax.div(j, 18)
    k = j - 18
    z = (1 - late) * (lax.div(j, 9) * 3) + late * (1 + lax.div(k, 2))
    rb = (1 - late) * lax.rem(j, 9) + late * (lax.rem(k, 2) * 8)
    return z, rb


def inner_tile(j):
    return 1 + lax.div(j, 7), 1 + lax.rem(j, 7)


def kernel(
    pop_hbm,
    kind_hbm,
    temp_hbm,
    line_hbm,
    want_hbm,
    place_hbm,
    hits_hbm,
    beam_hbm,
    out_hbm,
    temp_out_hbm,
    field,
    kind,
    temp,
    line,
    want,
    place,
    hits,
    beam,
    gas_pad,
    post1,
    post2,
    mask,
    vel,
    cells,
    ask_send,
    ask_recv,
    row_send,
    row_recv,
    heat_send,
    heat_recv,
    slot_hot,
    ray_hot,
    cell_hot,
    back_hot,
    ray_rows,
    live,
    thermal,
    temp_out,
    load_sem,
    small_sem,
    out_sem,
    gas_s,
    gas_r,
    halo_s,
    halo_r,
    all_s,
    all_r,
    th_s,
    th_r,
    row_sem,
):
    gz = lax.axis_index("gz")
    gy = lax.axis_index("gy")
    me = gz * N_GY + gy
    up, down = lax.rem(gz + 1, N_GZ), lax.rem(gz + N_GZ - 1, N_GZ)
    north, south = lax.rem(gy + 1, N_GY), lax.rem(gy + N_GY - 1, N_GY)

    barrier = pltpu.get_barrier_semaphore()

    def greet(i, carry):
        pl.semaphore_signal(
            barrier, 1, device_id=(lax.rem(gz + i, N_GZ), gy), device_id_type=MESH
        )
        return carry

    lax.fori_loop(1, N_GZ, greet, 0)
    for i in range(1, N_GY):
        pl.semaphore_signal(barrier, 1, device_id=(gz, lax.rem(gy + i, N_GY)), device_id_type=MESH)
    for peer in ((up, north), (up, south), (down, north), (down, south)):
        pl.semaphore_signal(barrier, 1, device_id=peer, device_id_type=MESH)

    small = []
    for i, (src, dst) in enumerate(
        (
            (kind_hbm, kind),
            (want_hbm, want),
            (line_hbm, line),
            (place_hbm, place),
            (hits_hbm, hits),
            (beam_hbm, beam),
            (temp_hbm, temp),
        )
    ):
        copy = pltpu.make_async_copy(src, dst, small_sem.at[i])
        copy.start()
        small.append(copy)

    def part(rb):
        rows = pl.ds(rb * 32, 32)
        return pltpu.make_async_copy(
            pop_hbm.at[:, rows], field.at[:, rows], load_sem.at[rb]
        )

    def start_part(rb, carry):
        part(rb).start()
        return carry

    lax.fori_loop(0, 9, start_part, 0)
    small[0].wait()

    def first(rb, carry):
        part(rb).wait()
        for z in range(DEPTH):
            rows = pl.ds(rb * 32 + z, 8, stride=DEPTH)
            gas = kind[rows, :] == 0
            gas_pad[z + 1, pl.ds(rb * 8 + PAD, 8), :] = gas.astype(jnp.int32)
            kept, velocity = collide([field[q, rows, :] for q in range(19)], gas)
            for q in range(19):
                post1[SLOT[q], z + 1, pl.ds(rb * 8 + PAD, 8), :] = kept[q]
            for i in range(4):
                vel[i, z, pl.ds(rb * 8, 8), :] = velocity[i]
        return carry

    lax.fori_loop(0, 9, first, 0)

    pl.semaphore_wait(barrier, N_GZ - 1 + N_GY - 1 + 4)

    low_src, low_dst = slice(PAD, PAD + 2), slice(PAD + ROWS, PAD + ROWS + 2)
    high_src, high_dst = slice(PAD + ROWS - 2, PAD + ROWS), slice(PAD - 2, PAD)
    body = slice(PAD, PAD + ROWS)
    planes = slice(1, 1 + DEPTH)

    def send(ref, src, dst, s, r, peer):
        copy = pltpu.make_async_remote_copy(
            src_ref=ref.at[src],
            dst_ref=ref.at[dst],
            send_sem=s,
            recv_sem=r,
            device_id=peer,
            device_id_type=MESH,
        )
        copy.start()
        return copy

    def halo(ref, first_sem):
        moves = (
            ((slice(0, 5), 4, body), (slice(0, 5), 0, body), (up, gy)),
            ((slice(5, 10), 1, body), (slice(5, 10), 5, body), (down, gy)),
            ((slice(4, 6), planes, high_src), (slice(4, 6), planes, high_dst), (gz, north)),
            ((slice(16, 19), planes, high_src), (slice(16, 19), planes, high_dst), (gz, north)),
            ((slice(9, 13), planes, low_src), (slice(9, 13), planes, low_dst), (gz, south)),
            ((slice(0, 1), planes, low_src), (slice(0, 1), planes, low_dst), (gz, south)),
            ((4, 4, high_src), (4, 0, high_dst), (up, north)),
            ((9, 1, low_src), (9, 5, low_dst), (down, south)),
            ((5, 1, high_src), (5, 5, high_dst), (down, north)),
            ((0, 4, low_src), (0, 0, low_dst), (up, south)),
        )
        return [
            send(ref, src, dst, halo_s.at[first_sem + i], halo_r.at[first_sem + i], peer)
            for i, (src, dst, peer) in enumerate(moves)
        ]

    gas_moves = (
        ((4, body), (0, body), (up, gy)),
        ((1, body), (5, body), (down, gy)),
        ((planes, high_src), (planes, high_dst), (gz, north)),
        ((planes, low_src), (planes, low_dst), (gz, south)),
        ((4, high_src), (0, high_dst), (up, north)),
        ((4, low_src), (0, low_dst), (up, south)),
        ((1, high_src), (5, high_dst), (down, north)),
        ((1, low_src), (5, low_dst), (down, south)),
    )
    gas_copies = [
        send(gas_pad, src, dst, gas_s.at[i], gas_r.at[i], peer)
        for i, (src, dst, peer) in enumerate(gas_moves)
    ]
    copies1 = halo(post1, 0)

    for i in range(1, N_GY):
        pl.semaphore_signal(row_sem, 1, device_id=(gz, lax.rem(gy + i, N_GY)), device_id_type=MESH)

    for copy in small[1:]:
        copy.wait()
    eye = tile_iota(0, (DEVICES, DEVICES)) == tile_iota(1, (DEVICES, DEVICES))
    lanes = tile_iota(1, (DEVICES, DEVICES))
    rows_of = jnp.zeros((DEVICES, DEVICES), jnp.float32)
    for s in range(CAP):
        asked = want[s : s + 1, :].astype(jnp.float32)
        column = jnp.sum(jnp.where(eye, asked, 0.0), axis=1, keepdims=True)
        rows_of = jnp.where(lanes == s, column, rows_of)
    ask_send[...] = rows_of
    ask_recv[pl.ds(me, 1), :] = ask_send[pl.ds(me, 1), :]
    pl.semaphore_wait(row_sem, N_GY - 1)

    def peer_of(i):
        p = lax.rem(me + i, DEVICES)
        return p, (lax.div(p, N_GY), lax.rem(p, N_GY))

    def ask(i, carry):
        p, peer = peer_of(i)
        pltpu.make_async_remote_copy(
            src_ref=ask_send.at[pl.ds(p, 1)],
            dst_ref=ask_recv.at[pl.ds(me, 1)],
            send_sem=all_s.at[0],
            recv_sem=all_r.at[0],
            device_id=peer,
            device_id_type=MESH,
        ).start()
        return carry

    lax.fori_loop(1, DEVICES, ask, 0)

    for copy in gas_copies:
        copy.wait()

    def masks(j, carry):
        z, rb = lax.div(j, 9), lax.rem(j, 9)
        place_x = lax.rem(
            (rb * 8 + tile_iota(0)) * 128 + tile_iota(1), jnp.full((8, 128), ACROSS, jnp.int32)
        )
        left, right = place_x == 0, place_x == ACROSS - 1
        own = gas_pad[z + 1, pl.ds(rb * 8 + PAD, 8), :]
        bits = own
        for q in range(1, 19):
            step_x, step_y, step_z = DIRS[q]
            source = shifted(window(gas_pad, (), z + 1 - step_z, rb), step_x, step_y, left, right)
            bits = bits | (jnp.maximum(source, own) << q)
        bits = bits | (left.astype(jnp.int32) << LEFT_BIT) | (right.astype(jnp.int32) << RIGHT_BIT)
        mask[z, pl.ds(rb * 8, 8), :] = bits
        return carry

    lax.fori_loop(0, 36, masks, 0)

    def second(tile):
        def step(j, carry):
            z, rb = tile(j)
            new, gas = passed(post1, mask, vel, z, rb)
            kept, velocity = collide(new, gas)
            for q in range(19):
                post2[SLOT[q], z + 1, pl.ds(rb * 8 + PAD, 8), :] = kept[q]
            for i in range(4):
                vel[i, z, pl.ds(rb * 8, 8), :] = velocity[i]
            return carry

        return step

    lax.fori_loop(0, 14, second(inner_tile), 0)
    for copy in copies1:
        copy.wait()
    lax.fori_loop(0, 22, second(edge_tile), 0)
    copies2 = halo(post2, 10)

    big0, big1 = tile_iota(0, (SLOTS, SLOTS)), tile_iota(1, (SLOTS, SLOTS))
    diagonal = big0 == big1
    spot = place[...]
    spot = (spot & 3) * DEVICES + (spot >> 2)
    slot_hot[...] = (big0 == spot).astype(jnp.float32).astype(jnp.bfloat16)
    spot_col = jnp.sum(
        jnp.where(diagonal, spot.astype(jnp.float32), 0.0), axis=1, keepdims=True
    )
    ray_hot[...] = (big1.astype(jnp.float32) == spot_col).astype(jnp.float32).astype(jnp.bfloat16)
    eye_rays = tile_iota(0, (RAYS, RAYS)) == tile_iota(1, (RAYS, RAYS))
    live[...] = jnp.broadcast_to(
        jnp.sum(jnp.where(eye_rays, hits[...].astype(jnp.float32), 0.0), axis=1, keepdims=True),
        (RAYS, 128),
    )
    pltpu.make_async_copy(
        ask_send.at[pl.ds(0, DEVICES - 1)], ask_recv.at[pl.ds(0, DEVICES - 1)], all_r.at[0]
    ).wait()
    block = tile_iota(1, (DEVICES, NB_DEV)).astype(jnp.float32)
    lines = line[...].astype(jnp.float32)
    wanted_row = []
    for s in range(CAP):
        chosen = ask_recv[:, s : s + 1] == block
        wanted_row.append(jnp.sum(jnp.where(chosen, lines, 0.0), axis=1, keepdims=True))
    row_col = jnp.concatenate(wanted_row, axis=0)
    cell_hot[...] = (
        (tile_iota(1, (SLOTS, 384)).astype(jnp.float32) == row_col)
        .astype(jnp.float32)
        .astype(jnp.bfloat16)
    )
    row_row = jnp.sum(jnp.where(diagonal, row_col, 0.0), axis=0, keepdims=True)
    back_hot[...] = (
        (tile_iota(0, (CELL_ROWS, SLOTS)).astype(jnp.float32) == row_row)
        .astype(jnp.float32)
        .astype(jnp.bfloat16)
    )
    cells[CELL_ROWS:, :] = jnp.zeros((384 - CELL_ROWS, 128), jnp.float32)

    def third(tile):
        def step(j, carry):
            z, rb = tile(j)
            new, gas = passed(post2, mask, vel, z, rb)
            rows = pl.ds(rb * 32 + z, 8, stride=DEPTH)
            for q in range(19):
                field[q, rows, :] = new[q]
            density, ux, uy, uz = moments(new)
            for i, v in enumerate((ux, uy, uz)):
                vel[i, z, pl.ds(rb * 8, 8), :] = v
            cosine = 0.2 + 0.7 / (1.0 + jnp.exp(-8.0 * (density - 1.0)))
            index = 1.0 + temp[rows, :]
            upper = (index - cosine) * (index - cosine) + 1.0
            lower = (index + cosine) * (index + cosine) + 1.0
            cells[pl.ds(pl.multiple_of(z * ROWS + rb * 8, 8), 8), :] = jnp.where(
                gas, 1.0, upper / lower
            )
            return carry

        return step

    lax.fori_loop(0, 14, third(inner_tile), 0)
    for copy in copies2:
        copy.wait()
    lax.fori_loop(0, 22, third(edge_tile), 0)
    lattice_copy = pltpu.make_async_copy(field, out_hbm, out_sem.at[0])
    lattice_copy.start()

    def to_all(src, dst, n):
        dst[:, pl.ds(me, 1), :] = src[:, pl.ds(me, 1), :]

        def one(i, carry):
            p, peer = peer_of(i)
            pltpu.make_async_remote_copy(
                src_ref=src.at[:, pl.ds(p, 1)],
                dst_ref=dst.at[:, pl.ds(me, 1)],
                send_sem=all_s.at[n],
                recv_sem=all_r.at[n],
                device_id=peer,
                device_id_type=MESH,
            ).start()
            return carry

        lax.fori_loop(1, DEVICES, one, 0)
        pltpu.make_async_copy(
            src.at[:, pl.ds(0, DEVICES - 1)], dst.at[:, pl.ds(0, DEVICES - 1)], all_r.at[n]
        ).wait()

    row_send[...] = pick(cell_hot[...], cells[...]).reshape(CAP, DEVICES, 128)
    to_all(row_send, row_recv, 1)

    ray_rows[...] = pick(ray_hot[...], row_recv[...].reshape(SLOTS, 128))
    energy = beam[...]
    hit_count = live[...]
    for j in range(BOUNCES):
        at = pl.ds(j, RAYS, stride=BOUNCES)
        ratio = ray_rows[at, :]
        ray_rows[at, :] = jnp.where(hit_count > float(j), energy * (1.0 - ratio), 0.0)
        energy = energy * ratio
    heat_send[...] = pick(slot_hot[...], ray_rows[...]).reshape(CAP, DEVICES, 128)
    to_all(heat_send, heat_recv, 2)

    cells[pl.ds(0, CELL_ROWS), :] = pick(back_hot[...], heat_recv[...].reshape(SLOTS, 128))

    def sources(j, carry):
        z, rb = lax.div(j, 9), lax.rem(j, 9)
        deposit = cells[pl.ds(pl.multiple_of(z * ROWS + rb * 8, 8), 8), :]
        source = temp[pl.ds(rb * 32 + z, 8, stride=DEPTH), :] + deposit
        eighth = 0.125 * source
        for i in range(3):
            moved = eighth * (4.0 * vel[i, z, pl.ds(rb * 8, 8), :])
            thermal[2 * i, z + 1, pl.ds(rb * 8 + PAD, 8), :] = eighth + moved
            thermal[2 * i + 1, z + 1, pl.ds(rb * 8 + PAD, 8), :] = eighth - moved
        cells[pl.ds(pl.multiple_of(z * ROWS + rb * 8, 8), 8), :] = 0.25 * source
        return carry

    lax.fori_loop(0, 36, sources, 0)
    th_moves = (
        ((4, 4, body), (4, 0, body), (up, gy)),
        ((5, 1, body), (5, 5, body), (down, gy)),
        ((2, planes, high_src), (2, planes, high_dst), (gz, north)),
        ((3, planes, low_src), (3, planes, low_dst), (gz, south)),
    )
    th_copies = [
        send(thermal, src, dst, th_s.at[i], th_r.at[i], peer)
        for i, (src, dst, peer) in enumerate(th_moves)
    ]
    for copy in th_copies:
        copy.wait()

    def gather(j, carry):
        z, rb = lax.div(j, 9), lax.rem(j, 9)
        bits = mask[z, pl.ds(rb * 8, 8), :]
        left = (bits & (1 << LEFT_BIT)) != 0
        right = (bits & (1 << RIGHT_BIT)) != 0
        total = cells[pl.ds(pl.multiple_of(z * ROWS + rb * 8, 8), 8), :]
        for i in range(6):
            step_x, step_y, step_z = DIRS[i + 1]
            total = total + shifted(
                window(thermal, (i,), z + 1 - step_z, rb), step_x, step_y, left, right
            )
        temp_out[pl.ds(rb * 32 + z, 8, stride=DEPTH), :] = total
        return carry

    lax.fori_loop(0, 36, gather, 0)
    last = pltpu.make_async_copy(temp_out, temp_out_hbm, out_sem.at[1])
    last.start()
    last.wait()
    lattice_copy.wait()
    pltpu.make_async_copy(
        ask_send.at[pl.ds(0, DEVICES - 1)], ask_recv.at[pl.ds(0, DEVICES - 1)], all_s.at[0]
    ).wait()
    for n, ref in ((1, row_send), (2, heat_send)):
        done = ref.at[:, pl.ds(0, DEVICES - 1)]
        pltpu.make_async_copy(done, done, all_s.at[n]).wait()


def fold(x):
    lead = x.shape[:-2]
    n = len(lead)
    x = x.reshape(lead + (DEPTH, ROWS, 128)).transpose(tuple(range(n)) + (n + 1, n, n + 2))
    return x.reshape(lead + (CELL_ROWS, 128))


def unfold(x):
    lead = x.shape[:-2]
    n = len(lead)
    x = x.reshape(lead + (ROWS, DEPTH, 128)).transpose(tuple(range(n)) + (n + 1, n, n + 2))
    return x.reshape(lead + (DEPTH, ROWS * 128))


def per_device(populations, kinds, temperature, lines, wanted, places, hits, beam):
    f32, i32, bf16 = jnp.float32, jnp.int32, jnp.bfloat16
    dma = pltpu.SemaphoreType.DMA
    lattice, heated = pl.pallas_call(
        kernel,
        out_shape=(
            jax.ShapeDtypeStruct((19, CELL_ROWS, 128), f32),
            jax.ShapeDtypeStruct((CELL_ROWS, 128), f32),
        ),
        in_specs=[pl.BlockSpec(memory_space=pl.ANY)] * 8,
        out_specs=[pl.BlockSpec(memory_space=pl.ANY)] * 2,
        scratch_shapes=[
            pltpu.VMEM((19, CELL_ROWS, 128), f32),
            pltpu.VMEM((CELL_ROWS, 128), i32),
            pltpu.VMEM((CELL_ROWS, 128), f32),
            pltpu.VMEM((1, NB_DEV), i32),
            pltpu.VMEM((CAP, DEVICES), i32),
            pltpu.VMEM((1, SLOTS), i32),
            pltpu.VMEM((1, RAYS), i32),
            pltpu.VMEM((RAYS, 128), f32),
            pltpu.VMEM((DEPTH + 2, PLANE, 128), i32),
            pltpu.VMEM((19, DEPTH + 2, PLANE, 128), f32),
            pltpu.VMEM((19, DEPTH + 2, PLANE, 128), f32),
            pltpu.VMEM((DEPTH, ROWS, 128), i32),
            pltpu.VMEM((4, DEPTH, ROWS, 128), f32),
            pltpu.VMEM((384, 128), f32),
            pltpu.VMEM((DEVICES, 128), f32),
            pltpu.VMEM((DEVICES, 128), f32),
            pltpu.VMEM((CAP, DEVICES, 128), f32),
            pltpu.VMEM((CAP, DEVICES, 128), f32),
            pltpu.VMEM((CAP, DEVICES, 128), f32),
            pltpu.VMEM((CAP, DEVICES, 128), f32),
            pltpu.VMEM((SLOTS, SLOTS), bf16),
            pltpu.VMEM((SLOTS, SLOTS), bf16),
            pltpu.VMEM((SLOTS, 384), bf16),
            pltpu.VMEM((CELL_ROWS, SLOTS), bf16),
            pltpu.VMEM((SLOTS, 128), f32),
            pltpu.VMEM((RAYS, 128), f32),
            pltpu.VMEM((6, DEPTH + 2, PLANE, 128), f32),
            pltpu.VMEM((CELL_ROWS, 128), f32),
            dma((9,)),
            dma((7,)),
            dma((2,)),
            dma((8,)),
            dma((8,)),
            dma((20,)),
            dma((20,)),
            dma((3,)),
            dma((3,)),
            dma((4,)),
            dma((4,)),
            pltpu.SemaphoreType.REGULAR,
        ],
        compiler_params=pltpu.CompilerParams(
            collective_id=0, has_side_effects=True, vmem_limit_bytes=56 * 2**20
        ),
        cost_estimate=pl.CostEstimate(
            flops=100_000_000, bytes_accessed=7_000_000, transcendentals=40_000
        ),
    )(
        fold(populations),
        fold(kinds),
        fold(temperature),
        lines,
        wanted[0].T,
        places,
        hits,
        beam[0],
    )
    return unfold(lattice), unfold(heated)


def solution(mesh):
    placed = (
        P(None, "gz", "gy"),
        P("gz", "gy"),
        P("gz", "gy"),
        P(("gz", "gy"), None),
        P(("gz", "gy"), None, None),
        P(("gz", "gy"), None),
        P(("gz", "gy"), None),
        P(("gz", "gy"), None, None),
    )
    return jax.shard_map(
        per_device,
        mesh=mesh,
        in_specs=placed,
        out_specs=(P(None, "gz", "gy"), P("gz", "gy")),
        check_vma=False,
    )
```

```python
import jax
import jax.numpy as jnp
from jax import lax
from jax.experimental import pallas as pl
from jax.experimental.pallas import tpu as pltpu
from jax.sharding import PartitionSpec as P

MESH = pl.DeviceIdType.MESH
N_GZ = 32
N_GY = 4
DEVICES = 128
CAP = 4
SLOTS = 512
NB_DEV = 64
RAYS = 64
BOUNCES = 8
ACROSS = 192
DEPTH = 4
ROWS = 72
CELL_ROWS = 288
PAD = 8
PLANE = ROWS + 2 * PAD

DIRS = [
    (0, 0, 0),
    (1, 0, 0),
    (-1, 0, 0),
    (0, 1, 0),
    (0, -1, 0),
    (0, 0, 1),
    (0, 0, -1),
    (1, 1, 0),
    (-1, -1, 0),
    (1, -1, 0),
    (-1, 1, 0),
    (1, 0, 1),
    (-1, 0, -1),
    (1, 0, -1),
    (-1, 0, 1),
    (0, 1, 1),
    (0, -1, -1),
    (0, 1, -1),
    (0, -1, 1),
]
WEIGHTS = [1.0 / 3.0] + [1.0 / 18.0] * 6 + [1.0 / 36.0] * 12
PAIRS = [(q, q + 1) for q in range(1, 19, 2)]
OPP = [0, 2, 1, 4, 3, 6, 5, 8, 7, 10, 9, 12, 11, 14, 13, 16, 15, 18, 17]
RELAX = 0.8
ORDER = [18, 5, 11, 14, 15, 17, 12, 13, 6, 16, 4, 8, 9, 1, 2, 0, 3, 7, 10]
SLOT = [ORDER.index(q) for q in range(19)]
LEFT_BIT = 19
RIGHT_BIT = 20


def tile_iota(axis, shape=(8, 128)):
    return lax.broadcasted_iota(jnp.int32, shape, axis)


def moments(f):
    d = {a: f[a] - f[b] for a, b in PAIRS}
    s = {a: f[a] + f[b] for a, b in PAIRS}
    density = (
        ((s[1] + s[3]) + (s[5] + s[7])) + ((s[9] + s[11]) + (s[13] + s[15])) + (s[17] + f[0])
    )
    mx = (d[1] + d[7]) + (d[9] + d[11]) + d[13]
    my = (d[3] + d[7]) + (d[15] - d[9]) + d[17]
    mz = (d[5] + d[11]) + (d[15] - d[13]) - d[17]
    inv = 1.0 / density
    return density, mx * inv, my * inv, mz * inv


def along(u, q):
    total = None
    for step, part in zip(DIRS[q], u):
        if step == 0:
            continue
        if total is None:
            total = part if step > 0 else -part
        else:
            total = total + part if step > 0 else total - part
    return total


def collide(f, gas):
    density, ux, uy, uz = moments(f)
    base = 1.0 - 1.5 * (ux * ux + uy * uy + uz * uz)
    triple = (3.0 * ux, 3.0 * uy, 3.0 * uz)
    kept = [None] * 19
    keep = 1.0 - RELAX
    scaled = {w: (RELAX * w) * density for w in (1.0 / 18.0, 1.0 / 36.0)}
    post = keep * f[0] + (RELAX / 3.0) * density * base
    kept[0] = jnp.where(gas, -f[0], post)
    for a, b in PAIRS:
        wd = scaled[WEIGHTS[a]]
        c = along(triple, a)
        even = wd * (base + 0.5 * (c * c))
        odd = wd * c
        kept[a] = jnp.where(gas, -f[b], keep * f[a] + (even + odd))
        kept[b] = jnp.where(gas, -f[a], keep * f[b] + (even - odd))
    zero = jnp.zeros_like(ux)
    velocity = [jnp.where(gas, zero, v) for v in (ux, uy, uz, base)]
    return kept, velocity


def shifted(load, step_x, step_y, left, right):
    lane = tile_iota(1)

    def flat(by):
        rows, lanes = by // 128, by % 128
        if lanes == 0:
            return load(-rows)
        picked = jnp.where(lane >= 128 - lanes, load(-rows - 1), load(-rows))
        return pltpu.roll(picked, lanes, 1)

    main = flat(step_x + ACROSS * step_y)
    if step_x == 0:
        return main
    by = step_x + ACROSS * step_y - ACROSS * step_x
    rows, lanes = by // 128, by % 128
    targets = (0, 64) if step_x == 1 else (63, 127)
    if all(t < lanes for t in targets):
        wrapped = pltpu.roll(load(-rows - 1), lanes, 1)
    elif all(t >= lanes for t in targets):
        wrapped = pltpu.roll(load(-rows), lanes, 1)
    else:
        wrapped = flat(by)
    return jnp.where(left if step_x == 1 else right, wrapped, main)


def window(ref, lead, z, rb):
    def load(n):
        return ref[(*lead, z, pl.ds(rb * 8 + (PAD + n), 8), slice(None))]

    return load


def passed(post_ref, mask_ref, vel_ref, z, rb):
    mask = mask_ref[z, pl.ds(rb * 8, 8), :]
    left = (mask & (1 << LEFT_BIT)) != 0
    right = (mask & (1 << RIGHT_BIT)) != 0
    ux, uy, uz, base = [vel_ref[i, z, pl.ds(rb * 8, 8), :] for i in range(4)]
    centre = [post_ref[SLOT[q], z + 1, pl.ds(rb * 8 + PAD, 8), :] for q in range(19)]
    new = [None] * 19
    new[0] = jnp.where((mask & 1) != 0, -centre[0], centre[0])
    triple = (3.0 * ux, 3.0 * uy, 3.0 * uz)
    for a, b in PAIRS:
        c = along(triple, a)
        both = (2.0 * WEIGHTS[a]) * (base + 0.5 * (c * c))
        for q, back in ((a, b), (b, a)):
            step_x, step_y, step_z = DIRS[q]
            source = shifted(
                window(post_ref, (SLOT[q],), z + 1 - step_z, rb), step_x, step_y, left, right
            )
            new[q] = jnp.where((mask & (1 << q)) != 0, both - centre[back], source)
    return new, (mask & 1) != 0


def two_terms(x):
    high = x.astype(jnp.bfloat16)
    low = (x - high.astype(jnp.float32)).astype(jnp.bfloat16)
    return jnp.concatenate([high, low], axis=1)


def pick(one_hot, values):
    both = jnp.dot(one_hot, two_terms(values), preferred_element_type=jnp.float32)
    return both[:, :128] + both[:, 128:]


def inner_tile(j):
    return 1 + lax.div(j, 7), 1 + lax.rem(j, 7)


def side_tile(j):
    return 1 + lax.div(j, 2), lax.rem(j, 2) * 8


def face_tile(third):
    return lambda j: (lax.div(j, 3) * 3, third * 3 + lax.rem(j, 3))


def any_tile(j):
    return lax.div(j, 9), lax.rem(j, 9)


def over(tile, count, body, unroll=None):
    def step(j, carry):
        body(*tile(j))
        return carry

    lax.fori_loop(0, count, step, 0, unroll=unroll or count)


def kernel(
    pop_hbm,
    kind_hbm,
    temp_hbm,
    line_hbm,
    want_hbm,
    place_hbm,
    hits_hbm,
    beam_hbm,
    field,
    thermal,
    cells,
    inputs,
    kind,
    temp,
    line,
    want,
    place,
    hits,
    beam,
    gas_pad,
    post1,
    post2,
    mask,
    vel,
    ask_send,
    ask_recv,
    row_send,
    row_recv,
    heat_send,
    heat_recv,
    slot_hot,
    ray_hot,
    cell_hot,
    back_hot,
    ray_rows,
    live,
    load_sem,
    small_sem,
    gas_s,
    gas_r,
    halo_s,
    halo_r,
    all_s,
    all_r,
    th_s,
    th_r,
    row_sem,
):
    gz = lax.axis_index("gz")
    gy = lax.axis_index("gy")
    me = gz * N_GY + gy
    up, down = lax.rem(gz + 1, N_GZ), lax.rem(gz + N_GZ - 1, N_GZ)
    north, south = lax.rem(gy + 1, N_GY), lax.rem(gy + N_GY - 1, N_GY)

    barrier = pltpu.get_barrier_semaphore()

    def greet(i, carry):
        pl.semaphore_signal(
            barrier, 1, device_id=(lax.rem(gz + i, N_GZ), gy), device_id_type=MESH
        )
        return carry

    lax.fori_loop(1, N_GZ, greet, 0)
    for i in range(1, N_GY):
        pl.semaphore_signal(barrier, 1, device_id=(gz, lax.rem(gy + i, N_GY)), device_id_type=MESH)
    for peer in ((up, north), (up, south), (down, north), (down, south)):
        pl.semaphore_signal(barrier, 1, device_id=peer, device_id_type=MESH)

    small = []
    for i, (src, dst) in enumerate(
        (
            (kind_hbm, kind),
            (want_hbm, want),
            (line_hbm, line),
            (place_hbm, place),
            (hits_hbm, hits),
            (beam_hbm, beam),
            (temp_hbm, temp),
        )
    ):
        copy = pltpu.make_async_copy(src, dst, small_sem.at[i])
        copy.start()
        small.append(copy)

    def part(rb):
        rows = pl.ds(rb * 32, 32)
        return pltpu.make_async_copy(pop_hbm.at[:, rows], inputs.at[:, rows], load_sem.at[rb])

    def start_part(rb, carry):
        part(rb).start()
        return carry

    lax.fori_loop(0, 9, start_part, 0)
    small[0].wait()

    def flags(z, rb):
        gas = kind[pl.ds(rb * 32 + z, 8, stride=DEPTH), :] == 0
        gas_pad[z + 1, pl.ds(rb * 8 + PAD, 8), :] = gas.astype(jnp.int32)

    over(any_tile, 36, flags, 12)

    low_src, low_dst = slice(PAD, PAD + 2), slice(PAD + ROWS, PAD + ROWS + 2)
    high_src, high_dst = slice(PAD + ROWS - 2, PAD + ROWS), slice(PAD - 2, PAD)
    body = slice(PAD, PAD + ROWS)
    planes = slice(1, 1 + DEPTH)

    def send(ref, src, dst, s, r, peer):
        copy = pltpu.make_async_remote_copy(
            src_ref=ref.at[src],
            dst_ref=ref.at[dst],
            send_sem=s,
            recv_sem=r,
            device_id=peer,
            device_id_type=MESH,
        )
        copy.start()
        return copy

    def face_moves(third):
        rows = slice(PAD + 24 * third, PAD + 24 * third + 24)
        return (
            ((slice(0, 5), 4, rows), (slice(0, 5), 0, rows), (up, gy)),
            ((slice(5, 10), 1, rows), (slice(5, 10), 5, rows), (down, gy)),
        )

    side_moves = (
        ((slice(4, 6), planes, high_src), (slice(4, 6), planes, high_dst), (gz, north)),
        ((slice(16, 19), planes, high_src), (slice(16, 19), planes, high_dst), (gz, north)),
        ((slice(9, 13), planes, low_src), (slice(9, 13), planes, low_dst), (gz, south)),
        ((slice(0, 1), planes, low_src), (slice(0, 1), planes, low_dst), (gz, south)),
    )
    corner_moves = (
        ((4, 4, high_src), (4, 0, high_dst), (up, north)),
        ((9, 1, low_src), (9, 5, low_dst), (down, south)),
        ((5, 1, high_src), (5, 5, high_dst), (down, north)),
        ((0, 4, low_src), (0, 0, low_dst), (up, south)),
    )

    def send_all(ref, moves, s, r, first_sem):
        return [
            send(ref, src, dst, s.at[first_sem + i], r.at[first_sem + i], peer)
            for i, (src, dst, peer) in enumerate(moves)
        ]

    gas_moves = (
        ((4, body), (0, body), (up, gy)),
        ((1, body), (5, body), (down, gy)),
        ((planes, high_src), (planes, high_dst), (gz, north)),
        ((planes, low_src), (planes, low_dst), (gz, south)),
        ((4, high_src), (0, high_dst), (up, north)),
        ((4, low_src), (0, low_dst), (up, south)),
        ((1, high_src), (5, high_dst), (down, north)),
        ((1, low_src), (5, low_dst), (down, south)),
    )

    def first(z, rb):
        rows = pl.ds(rb * 32 + z, 8, stride=DEPTH)
        kept, velocity = collide([inputs[q, rows, :] for q in range(19)], kind[rows, :] == 0)
        for q in range(19):
            post1[SLOT[q], z + 1, pl.ds(rb * 8 + PAD, 8), :] = kept[q]
        for i in range(4):
            vel[i, z, pl.ds(rb * 8, 8), :] = velocity[i]

    faces1, gas_copies = [], []
    for third in range(3):
        for rb in range(3 * third, 3 * third + 3):
            part(rb).wait()
        over(lambda j: (lax.div(j, 3), 3 * third + lax.rem(j, 3)), 12, first)
        if third == 0:
            pl.semaphore_wait(barrier, N_GZ - 1 + N_GY - 1 + 4)
        faces1 += send_all(post1, face_moves(third), halo_s, halo_r, 2 * third)
        if third == 0:
            gas_copies += send_all(gas_pad, gas_moves[:2], gas_s, gas_r, 0)
        if third == 1:
            gas_copies += send_all(gas_pad, gas_moves[2:], gas_s, gas_r, 2)
    sides1 = send_all(post1, side_moves, halo_s, halo_r, 6)
    corners1 = send_all(post1, corner_moves, halo_s, halo_r, 10)

    for i in range(1, N_GY):
        pl.semaphore_signal(row_sem, 1, device_id=(gz, lax.rem(gy + i, N_GY)), device_id_type=MESH)

    for copy in small[1:]:
        copy.wait()
    eye = tile_iota(0, (DEVICES, DEVICES)) == tile_iota(1, (DEVICES, DEVICES))
    lanes = tile_iota(1, (DEVICES, DEVICES))
    rows_of = jnp.zeros((DEVICES, DEVICES), jnp.float32)
    for s in range(CAP):
        asked = want[s : s + 1, :].astype(jnp.float32)
        column = jnp.sum(jnp.where(eye, asked, 0.0), axis=1, keepdims=True)
        rows_of = jnp.where(lanes == s, column, rows_of)
    ask_send[...] = rows_of
    ask_recv[pl.ds(me, 1), :] = ask_send[pl.ds(me, 1), :]
    pl.semaphore_wait(row_sem, N_GY - 1)

    def peer_of(i):
        def onward(own, k):
            return lax.rem(own + 10 - lax.div(k * (k + 1), 2), 4)

        x = onward(lax.div(gz, 8), lax.div(i, 32))
        y = onward(lax.rem(lax.div(gz, 2), 4), lax.rem(lax.div(i, 8), 4))
        z = onward(gy, lax.rem(lax.div(i, 2), 4))
        core = lax.rem(gz + 1 + lax.rem(i, 2), 2)
        column = (x * 4 + y) * 2 + core
        return column * N_GY + z, (column, z)

    def ask(i, carry):
        p, peer = peer_of(i)
        pltpu.make_async_remote_copy(
            src_ref=ask_send.at[pl.ds(p, 1)],
            dst_ref=ask_recv.at[pl.ds(me, 1)],
            send_sem=all_s.at[0],
            recv_sem=all_r.at[0],
            device_id=peer,
            device_id_type=MESH,
        ).start()
        return carry

    lax.fori_loop(0, DEVICES - 1, ask, 0)

    def masks(z, rb):
        place_x = lax.rem(
            (rb * 8 + tile_iota(0)) * 128 + tile_iota(1), jnp.full((8, 128), ACROSS, jnp.int32)
        )
        left, right = place_x == 0, place_x == ACROSS - 1
        own = gas_pad[z + 1, pl.ds(rb * 8 + PAD, 8), :]
        bits = own
        for q in range(1, 19):
            step_x, step_y, step_z = DIRS[q]
            source = shifted(window(gas_pad, (), z + 1 - step_z, rb), step_x, step_y, left, right)
            bits = bits | (jnp.maximum(source, own) << q)
        bits = bits | (left.astype(jnp.int32) << LEFT_BIT) | (right.astype(jnp.int32) << RIGHT_BIT)
        mask[z, pl.ds(rb * 8, 8), :] = bits

    def second(z, rb):
        new, gas = passed(post1, mask, vel, z, rb)
        kept, velocity = collide(new, gas)
        for q in range(19):
            post2[SLOT[q], z + 1, pl.ds(rb * 8 + PAD, 8), :] = kept[q]
        for i in range(4):
            vel[i, z, pl.ds(rb * 8, 8), :] = velocity[i]

    over(inner_tile, 14, masks, 7)
    over(inner_tile, 14, second, 7)
    for copy in gas_copies:
        copy.wait()
    over(side_tile, 4, masks)
    for third in range(3):
        over(face_tile(third), 6, masks)
    for copy in sides1:
        copy.wait()
    over(side_tile, 4, second)
    for copy in faces1 + corners1:
        copy.wait()
    faces2 = []
    for third in range(3):
        over(face_tile(third), 6, second)
        faces2 += send_all(post2, face_moves(third), halo_s, halo_r, 14 + 2 * third)
    corners2 = send_all(post2, corner_moves, halo_s, halo_r, 24)
    sides2 = send_all(post2, side_moves, halo_s, halo_r, 20)

    big0, big1 = tile_iota(0, (SLOTS, SLOTS)), tile_iota(1, (SLOTS, SLOTS))
    diagonal = big0 == big1
    spot = place[...]
    spot = (spot & 3) * DEVICES + (spot >> 2)
    slot_hot[...] = (big0 == spot).astype(jnp.float32).astype(jnp.bfloat16)
    spot_col = jnp.sum(
        jnp.where(diagonal, spot.astype(jnp.float32), 0.0), axis=1, keepdims=True
    )
    ray_hot[...] = (big1.astype(jnp.float32) == spot_col).astype(jnp.float32).astype(jnp.bfloat16)
    eye_rays = tile_iota(0, (RAYS, RAYS)) == tile_iota(1, (RAYS, RAYS))
    live[...] = jnp.broadcast_to(
        jnp.sum(jnp.where(eye_rays, hits[...].astype(jnp.float32), 0.0), axis=1, keepdims=True),
        (RAYS, 128),
    )
    pltpu.make_async_copy(
        ask_send.at[pl.ds(0, DEVICES - 1)], ask_recv.at[pl.ds(0, DEVICES - 1)], all_r.at[0]
    ).wait()
    block = tile_iota(1, (DEVICES, NB_DEV)).astype(jnp.float32)
    lines = line[...].astype(jnp.float32)
    wanted_row = []
    for s in range(CAP):
        chosen = ask_recv[:, s : s + 1] == block
        wanted_row.append(jnp.sum(jnp.where(chosen, lines, 0.0), axis=1, keepdims=True))
    row_col = jnp.concatenate(wanted_row, axis=0)
    cell_hot[...] = (
        (tile_iota(1, (SLOTS, 384)).astype(jnp.float32) == row_col)
        .astype(jnp.float32)
        .astype(jnp.bfloat16)
    )
    row_row = jnp.sum(jnp.where(diagonal, row_col, 0.0), axis=0, keepdims=True)
    back_hot[...] = (
        (tile_iota(0, (CELL_ROWS, SLOTS)).astype(jnp.float32) == row_row)
        .astype(jnp.float32)
        .astype(jnp.bfloat16)
    )
    cells[CELL_ROWS:, :] = jnp.zeros((384 - CELL_ROWS, 128), jnp.float32)

    def last(z, rb):
        new, gas = passed(post2, mask, vel, z, rb)
        rows = pl.ds(rb * 32 + z, 8, stride=DEPTH)
        for q in range(19):
            field[q, rows, :] = new[q]
        density, ux, uy, uz = moments(new)
        for i, v in enumerate((ux, uy, uz)):
            vel[i, z, pl.ds(rb * 8, 8), :] = v
        cosine = 0.2 + 0.7 / (1.0 + jnp.exp(-8.0 * (density - 1.0)))
        index = 1.0 + temp[rows, :]
        upper = (index - cosine) * (index - cosine) + 1.0
        lower = (index + cosine) * (index + cosine) + 1.0
        cells[pl.ds(pl.multiple_of(z * ROWS + rb * 8, 8), 8), :] = jnp.where(
            gas, 1.0, upper / lower
        )

    over(inner_tile, 14, last, 7)
    for copy in sides2:
        copy.wait()
    over(side_tile, 4, last)
    for copy in faces2 + corners2:
        copy.wait()
    for third in range(3):
        over(face_tile(third), 6, last)

    def to_all(src, dst, n):
        dst[:, pl.ds(me, 1), :] = src[:, pl.ds(me, 1), :]

        def one(i, carry):
            p, peer = peer_of(i)
            pltpu.make_async_remote_copy(
                src_ref=src.at[:, pl.ds(p, 1)],
                dst_ref=dst.at[:, pl.ds(me, 1)],
                send_sem=all_s.at[n],
                recv_sem=all_r.at[n],
                device_id=peer,
                device_id_type=MESH,
            ).start()
            return carry

        lax.fori_loop(0, DEVICES - 1, one, 0)
        pltpu.make_async_copy(
            src.at[:, pl.ds(0, DEVICES - 1)], dst.at[:, pl.ds(0, DEVICES - 1)], all_r.at[n]
        ).wait()

    row_send[...] = pick(cell_hot[...], cells[...]).reshape(CAP, DEVICES, 128)
    to_all(row_send, row_recv, 1)

    ray_rows[...] = pick(ray_hot[...], row_recv[...].reshape(SLOTS, 128))
    energy = beam[...]
    hit_count = live[...]
    for j in range(BOUNCES):
        at = pl.ds(j, RAYS, stride=BOUNCES)
        ratio = ray_rows[at, :]
        ray_rows[at, :] = jnp.where(hit_count > float(j), energy * (1.0 - ratio), 0.0)
        energy = energy * ratio
    heat_send[...] = pick(slot_hot[...], ray_rows[...]).reshape(CAP, DEVICES, 128)
    to_all(heat_send, heat_recv, 2)

    cells[pl.ds(0, CELL_ROWS), :] = pick(back_hot[...], heat_recv[...].reshape(SLOTS, 128))

    def sources(z, rb):
        at = pl.ds(pl.multiple_of(z * ROWS + rb * 8, 8), 8)
        source = temp[pl.ds(rb * 32 + z, 8, stride=DEPTH), :] + cells[at, :]
        eighth = 0.125 * source
        for i in range(3):
            moved = eighth * (4.0 * vel[i, z, pl.ds(rb * 8, 8), :])
            thermal[2 * i, z + 1, pl.ds(rb * 8 + PAD, 8), :] = eighth + moved
            thermal[2 * i + 1, z + 1, pl.ds(rb * 8 + PAD, 8), :] = eighth - moved
        cells[at, :] = 0.25 * source

    over(any_tile, 36, sources, 12)
    th_moves = (
        ((4, 4, body), (4, 0, body), (up, gy)),
        ((5, 1, body), (5, 5, body), (down, gy)),
        ((2, planes, high_src), (2, planes, high_dst), (gz, north)),
        ((3, planes, low_src), (3, planes, low_dst), (gz, south)),
    )
    for copy in send_all(thermal, th_moves, th_s, th_r, 0):
        copy.wait()
    pltpu.make_async_copy(
        ask_send.at[pl.ds(0, DEVICES - 1)], ask_recv.at[pl.ds(0, DEVICES - 1)], all_s.at[0]
    ).wait()
    for n, ref in ((1, row_send), (2, heat_send)):
        done = ref.at[:, pl.ds(0, DEVICES - 1)]
        pltpu.make_async_copy(done, done, all_s.at[n]).wait()


def finish(field, thermal, cells, out_hbm, temp_out_hbm, temp_out, out_sem, temp_sem):
    copies = []
    for i, (lo, hi) in enumerate(((0, 5), (5, 10), (10, 15), (15, 19))):
        copy = pltpu.make_async_copy(field.at[lo:hi], out_hbm.at[lo:hi], out_sem.at[i])
        copy.start()
        copies.append(copy)

    def gather(z, rb):
        place_x = lax.rem(
            (rb * 8 + tile_iota(0)) * 128 + tile_iota(1), jnp.full((8, 128), ACROSS, jnp.int32)
        )
        left, right = place_x == 0, place_x == ACROSS - 1
        total = cells[pl.ds(pl.multiple_of(z * ROWS + rb * 8, 8), 8), :]
        for i in range(6):
            step_x, step_y, step_z = DIRS[i + 1]
            total = total + shifted(
                window(thermal, (i,), z + 1 - step_z, rb), step_x, step_y, left, right
            )
        temp_out[pl.ds(rb * 32 + z, 8, stride=DEPTH), :] = total

    over(lambda j: (lax.rem(j, 4), lax.div(j, 4)), 36, gather, 12)
    copy = pltpu.make_async_copy(temp_out, temp_out_hbm, temp_sem)
    copy.start()
    copy.wait()
    for copy in copies:
        copy.wait()


def fold(x):
    lead = x.shape[:-2]
    n = len(lead)
    x = x.reshape(lead + (DEPTH, ROWS, 128)).transpose(tuple(range(n)) + (n + 1, n, n + 2))
    return x.reshape(lead + (CELL_ROWS, 128))


def unfold(x):
    lead = x.shape[:-2]
    n = len(lead)
    x = x.reshape(lead + (ROWS, DEPTH, 128)).transpose(tuple(range(n)) + (n + 1, n, n + 2))
    return x.reshape(lead + (DEPTH, ROWS * 128))


def per_device(populations, kinds, temperature, lines, wanted, places, hits, beam):
    f32, i32, bf16 = jnp.float32, jnp.int32, jnp.bfloat16
    dma = pltpu.SemaphoreType.DMA
    vmem = pl.BlockSpec(memory_space=pltpu.VMEM)
    whole = pl.BlockSpec(memory_space=pl.ANY)
    operands = (
        fold(populations),
        fold(kinds),
        fold(temperature),
        lines,
        wanted[0].T,
        places,
        hits,
        beam[0],
    )
    field, thermal, cells = pl.pallas_call(
        kernel,
        out_shape=(
            pltpu.VMEM((19, CELL_ROWS, 128), f32),
            pltpu.VMEM((6, DEPTH + 2, PLANE, 128), f32),
            pltpu.VMEM((384, 128), f32),
        ),
        in_specs=[whole] * 8,
        out_specs=[vmem] * 3,
        scratch_shapes=[
            pltpu.VMEM((19, CELL_ROWS, 128), f32),
            pltpu.VMEM((CELL_ROWS, 128), i32),
            pltpu.VMEM((CELL_ROWS, 128), f32),
            pltpu.VMEM((1, NB_DEV), i32),
            pltpu.VMEM((CAP, DEVICES), i32),
            pltpu.VMEM((1, SLOTS), i32),
            pltpu.VMEM((1, RAYS), i32),
            pltpu.VMEM((RAYS, 128), f32),
            pltpu.VMEM((DEPTH + 2, PLANE, 128), i32),
            pltpu.VMEM((19, DEPTH + 2, PLANE, 128), f32),
            pltpu.VMEM((19, DEPTH + 2, PLANE, 128), f32),
            pltpu.VMEM((DEPTH, ROWS, 128), i32),
            pltpu.VMEM((4, DEPTH, ROWS, 128), f32),
            pltpu.VMEM((DEVICES, 128), f32),
            pltpu.VMEM((DEVICES, 128), f32),
            pltpu.VMEM((CAP, DEVICES, 128), f32),
            pltpu.VMEM((CAP, DEVICES, 128), f32),
            pltpu.VMEM((CAP, DEVICES, 128), f32),
            pltpu.VMEM((CAP, DEVICES, 128), f32),
            pltpu.VMEM((SLOTS, SLOTS), bf16),
            pltpu.VMEM((SLOTS, SLOTS), bf16),
            pltpu.VMEM((SLOTS, 384), bf16),
            pltpu.VMEM((CELL_ROWS, SLOTS), bf16),
            pltpu.VMEM((SLOTS, 128), f32),
            pltpu.VMEM((RAYS, 128), f32),
            dma((9,)),
            dma((7,)),
            dma((8,)),
            dma((8,)),
            dma((28,)),
            dma((28,)),
            dma((3,)),
            dma((3,)),
            dma((4,)),
            dma((4,)),
            pltpu.SemaphoreType.REGULAR,
        ],
        compiler_params=pltpu.CompilerParams(
            collective_id=0, has_side_effects=True, vmem_limit_bytes=40 * 2**20
        ),
        cost_estimate=pl.CostEstimate(
            flops=100_000_000, bytes_accessed=7_000_000, transcendentals=40_000
        ),
    )(*[pltpu.with_memory_space_constraint(x, pltpu.HBM) for x in operands])
    lattice, heated = pl.pallas_call(
        finish,
        out_shape=(
            jax.ShapeDtypeStruct((19, CELL_ROWS, 128), f32),
            jax.ShapeDtypeStruct((CELL_ROWS, 128), f32),
        ),
        in_specs=[vmem] * 3,
        out_specs=[whole] * 2,
        scratch_shapes=[pltpu.VMEM((CELL_ROWS, 128), f32), dma((4,)), dma],
        compiler_params=pltpu.CompilerParams(vmem_limit_bytes=40 * 2**20),
        cost_estimate=pl.CostEstimate(
            flops=1_000_000, bytes_accessed=7_000_000, transcendentals=0
        ),
    )(*[pltpu.with_memory_space_constraint(x, pltpu.VMEM) for x in (field, thermal, cells)])
    return unfold(lattice), unfold(heated)


def solution(mesh):
    placed = (
        P(None, "gz", "gy"),
        P("gz", "gy"),
        P("gz", "gy"),
        P(("gz", "gy"), None),
        P(("gz", "gy"), None, None),
        P(("gz", "gy"), None),
        P(("gz", "gy"), None),
        P(("gz", "gy"), None, None),
    )
    return jax.shard_map(
        per_device,
        mesh=mesh,
        in_specs=placed,
        out_specs=(P(None, "gz", "gy"), P("gz", "gy")),
        check_vma=False,
    )
```

```python
import jax
import jax.numpy as jnp
from jax import lax
from jax.experimental import pallas as pl
from jax.experimental.pallas import tpu as pltpu
from jax.sharding import PartitionSpec as P

MESH = pl.DeviceIdType.MESH
N_GZ = 32
N_GY = 4
DEVICES = 128
CAP = 4
SLOTS = 512
NB_DEV = 64
RAYS = 64
BOUNCES = 8
ACROSS = 192
DEPTH = 4
ROWS = 72
CELL_ROWS = 288
PAD = 8
PLANE = ROWS + 2 * PAD

DIRS = [
    (0, 0, 0),
    (1, 0, 0),
    (-1, 0, 0),
    (0, 1, 0),
    (0, -1, 0),
    (0, 0, 1),
    (0, 0, -1),
    (1, 1, 0),
    (-1, -1, 0),
    (1, -1, 0),
    (-1, 1, 0),
    (1, 0, 1),
    (-1, 0, -1),
    (1, 0, -1),
    (-1, 0, 1),
    (0, 1, 1),
    (0, -1, -1),
    (0, 1, -1),
    (0, -1, 1),
]
WEIGHTS = [1.0 / 3.0] + [1.0 / 18.0] * 6 + [1.0 / 36.0] * 12
PAIRS = [(q, q + 1) for q in range(1, 19, 2)]
OPP = [0, 2, 1, 4, 3, 6, 5, 8, 7, 10, 9, 12, 11, 14, 13, 16, 15, 18, 17]
RELAX = 0.8
ORDER = [18, 5, 11, 14, 15, 17, 12, 13, 6, 16, 4, 8, 9, 1, 2, 0, 3, 7, 10]
SLOT = [ORDER.index(q) for q in range(19)]
LEFT_BIT = 19
RIGHT_BIT = 20


def tile_iota(axis, shape=(8, 128)):
    return lax.broadcasted_iota(jnp.int32, shape, axis)


def moments(f):
    d = {a: f[a] - f[b] for a, b in PAIRS}
    s = {a: f[a] + f[b] for a, b in PAIRS}
    density = (
        ((s[1] + s[3]) + (s[5] + s[7])) + ((s[9] + s[11]) + (s[13] + s[15])) + (s[17] + f[0])
    )
    mx = (d[1] + d[7]) + (d[9] + d[11]) + d[13]
    my = (d[3] + d[7]) + (d[15] - d[9]) + d[17]
    mz = (d[5] + d[11]) + (d[15] - d[13]) - d[17]
    inv = 1.0 / density
    return density, mx * inv, my * inv, mz * inv


def along(u, q):
    total = None
    for step, part in zip(DIRS[q], u):
        if step == 0:
            continue
        if total is None:
            total = part if step > 0 else -part
        else:
            total = total + part if step > 0 else total - part
    return total


def collide(f, gas):
    density, ux, uy, uz = moments(f)
    base = 1.0 - 1.5 * (ux * ux + uy * uy + uz * uz)
    triple = (3.0 * ux, 3.0 * uy, 3.0 * uz)
    kept = [None] * 19
    keep = 1.0 - RELAX
    scaled = {w: (RELAX * w) * density for w in (1.0 / 18.0, 1.0 / 36.0)}
    post = keep * f[0] + (RELAX / 3.0) * density * base
    kept[0] = jnp.where(gas, -f[0], post)
    for a, b in PAIRS:
        wd = scaled[WEIGHTS[a]]
        c = along(triple, a)
        even = wd * (base + 0.5 * (c * c))
        odd = wd * c
        kept[a] = jnp.where(gas, -f[b], keep * f[a] + (even + odd))
        kept[b] = jnp.where(gas, -f[a], keep * f[b] + (even - odd))
    zero = jnp.zeros_like(ux)
    velocity = [jnp.where(gas, zero, v) for v in (ux, uy, uz, base)]
    return kept, velocity


def shifted(load, step_x, step_y, left, right):
    lane = tile_iota(1)

    def flat(by):
        rows, lanes = by // 128, by % 128
        if lanes == 0:
            return load(-rows)
        picked = jnp.where(lane >= 128 - lanes, load(-rows - 1), load(-rows))
        return pltpu.roll(picked, lanes, 1)

    main = flat(step_x + ACROSS * step_y)
    if step_x == 0:
        return main
    by = step_x + ACROSS * step_y - ACROSS * step_x
    rows, lanes = by // 128, by % 128
    targets = (0, 64) if step_x == 1 else (63, 127)
    if all(t < lanes for t in targets):
        wrapped = pltpu.roll(load(-rows - 1), lanes, 1)
    elif all(t >= lanes for t in targets):
        wrapped = pltpu.roll(load(-rows), lanes, 1)
    else:
        wrapped = flat(by)
    return jnp.where(left if step_x == 1 else right, wrapped, main)


def window(ref, lead, z, rb):
    def load(n):
        return ref[(*lead, z, pl.ds(rb * 8 + (PAD + n), 8), slice(None))]

    return load


def passed(post_ref, mask_ref, vel_ref, z, rb):
    mask = mask_ref[z, pl.ds(rb * 8, 8), :]
    left = (mask & (1 << LEFT_BIT)) != 0
    right = (mask & (1 << RIGHT_BIT)) != 0
    ux, uy, uz, base = [vel_ref[i, z, pl.ds(rb * 8, 8), :] for i in range(4)]
    centre = [post_ref[SLOT[q], z + 1, pl.ds(rb * 8 + PAD, 8), :] for q in range(19)]
    new = [None] * 19
    new[0] = jnp.where((mask & 1) != 0, -centre[0], centre[0])
    triple = (3.0 * ux, 3.0 * uy, 3.0 * uz)
    for a, b in PAIRS:
        c = along(triple, a)
        both = (2.0 * WEIGHTS[a]) * (base + 0.5 * (c * c))
        for q, back in ((a, b), (b, a)):
            step_x, step_y, step_z = DIRS[q]
            source = shifted(
                window(post_ref, (SLOT[q],), z + 1 - step_z, rb), step_x, step_y, left, right
            )
            new[q] = jnp.where((mask & (1 << q)) != 0, both - centre[back], source)
    return new, (mask & 1) != 0


def two_terms(x):
    high = x.astype(jnp.bfloat16)
    low = (x - high.astype(jnp.float32)).astype(jnp.bfloat16)
    return jnp.concatenate([high, low], axis=1)


def pick(one_hot, values):
    both = jnp.dot(one_hot, two_terms(values), preferred_element_type=jnp.float32)
    return both[:, :128] + both[:, 128:]


def inner_tile(j):
    return 1 + lax.div(j, 7), 1 + lax.rem(j, 7)


def side_tile(j):
    return 1 + lax.div(j, 2), lax.rem(j, 2) * 8


def face_tile(third):
    return lambda j: (lax.div(j, 3) * 3, third * 3 + lax.rem(j, 3))


def any_tile(j):
    return lax.div(j, 9), lax.rem(j, 9)


def over(tile, count, body, unroll=None):
    def step(j, carry):
        body(*tile(j))
        return carry

    lax.fori_loop(0, count, step, 0, unroll=unroll or count)


def kernel(
    pop_hbm,
    kind_hbm,
    temp_hbm,
    line_hbm,
    want_hbm,
    place_hbm,
    hits_hbm,
    beam_hbm,
    field,
    thermal,
    cells,
    inputs,
    kind,
    temp,
    line,
    want,
    place,
    hits,
    beam,
    gas_pad,
    post1,
    post2,
    mask,
    vel,
    ask_send,
    ask_mid,
    ask_recv,
    row_send,
    row_recv,
    heat_send,
    heat_recv,
    slot_hot,
    ray_hot,
    cell_hot,
    back_hot,
    ray_rows,
    live,
    load_sem,
    small_sem,
    gas_s,
    gas_r,
    halo_s,
    halo_r,
    all_s,
    all_r,
    th_s,
    th_r,
):
    gz = lax.axis_index("gz")
    gy = lax.axis_index("gy")
    up, down = lax.rem(gz + 1, N_GZ), lax.rem(gz + N_GZ - 1, N_GZ)
    north, south = lax.rem(gy + 1, N_GY), lax.rem(gy + N_GY - 1, N_GY)

    kind_copy = pltpu.make_async_copy(kind_hbm, kind, small_sem.at[6])
    kind_copy.start()

    def part(rb):
        rows = pl.ds(rb * 32, 32)
        return pltpu.make_async_copy(pop_hbm.at[:, rows], inputs.at[:, rows], load_sem.at[rb])

    def start_part(rb, carry):
        part(rb).start()
        return carry

    lax.fori_loop(0, 9, start_part, 0, unroll=9)

    small = []
    for i, (src, dst) in enumerate(
        (
            (want_hbm, want),
            (line_hbm, line),
            (place_hbm, place),
            (hits_hbm, hits),
            (beam_hbm, beam),
            (temp_hbm, temp),
        )
    ):
        copy = pltpu.make_async_copy(src, dst, small_sem.at[i])
        copy.start()
        small.append(copy)

    barrier = pltpu.get_barrier_semaphore()

    def greet(i, carry):
        pl.semaphore_signal(
            barrier, 1, device_id=(lax.rem(gz + i, N_GZ), gy), device_id_type=MESH
        )
        return carry

    lax.fori_loop(1, N_GZ, greet, 0, unroll=N_GZ - 1)
    for i in range(1, N_GY):
        pl.semaphore_signal(barrier, 1, device_id=(gz, lax.rem(gy + i, N_GY)), device_id_type=MESH)
    for peer in ((up, north), (up, south), (down, north), (down, south)):
        pl.semaphore_signal(barrier, 1, device_id=peer, device_id_type=MESH)

    kind_copy.wait()

    def flags(z, rb):
        gas = kind[pl.ds(rb * 32 + z, 8, stride=DEPTH), :] == 0
        gas_pad[z + 1, pl.ds(rb * 8 + PAD, 8), :] = gas.astype(jnp.int32)

    over(any_tile, 36, flags, 12)

    low_src, low_dst = slice(PAD, PAD + 2), slice(PAD + ROWS, PAD + ROWS + 2)
    high_src, high_dst = slice(PAD + ROWS - 2, PAD + ROWS), slice(PAD - 2, PAD)
    body = slice(PAD, PAD + ROWS)
    planes = slice(1, 1 + DEPTH)

    def send(ref, src, dst, s, r, peer):
        copy = pltpu.make_async_remote_copy(
            src_ref=ref.at[src],
            dst_ref=ref.at[dst],
            send_sem=s,
            recv_sem=r,
            device_id=peer,
            device_id_type=MESH,
        )
        copy.start()
        return copy

    def face_moves(third):
        rows = slice(PAD + 24 * third, PAD + 24 * third + 24)
        return (
            ((slice(0, 5), 4, rows), (slice(0, 5), 0, rows), (up, gy)),
            ((slice(5, 10), 1, rows), (slice(5, 10), 5, rows), (down, gy)),
        )

    side_moves = (
        ((slice(4, 6), planes, high_src), (slice(4, 6), planes, high_dst), (gz, north)),
        ((slice(16, 19), planes, high_src), (slice(16, 19), planes, high_dst), (gz, north)),
        ((slice(9, 13), planes, low_src), (slice(9, 13), planes, low_dst), (gz, south)),
        ((slice(0, 1), planes, low_src), (slice(0, 1), planes, low_dst), (gz, south)),
    )
    corner_moves = (
        ((4, 4, high_src), (4, 0, high_dst), (up, north)),
        ((9, 1, low_src), (9, 5, low_dst), (down, south)),
        ((5, 1, high_src), (5, 5, high_dst), (down, north)),
        ((0, 4, low_src), (0, 0, low_dst), (up, south)),
    )

    def send_all(ref, moves, s, r, first_sem):
        return [
            send(ref, src, dst, s.at[first_sem + i], r.at[first_sem + i], peer)
            for i, (src, dst, peer) in enumerate(moves)
        ]

    gas_moves = (
        ((4, body), (0, body), (up, gy)),
        ((1, body), (5, body), (down, gy)),
        ((planes, high_src), (planes, high_dst), (gz, north)),
        ((planes, low_src), (planes, low_dst), (gz, south)),
        ((4, high_src), (0, high_dst), (up, north)),
        ((4, low_src), (0, low_dst), (up, south)),
        ((1, high_src), (5, high_dst), (down, north)),
        ((1, low_src), (5, low_dst), (down, south)),
    )

    def first(z, rb):
        rows = pl.ds(rb * 32 + z, 8, stride=DEPTH)
        kept, velocity = collide([inputs[q, rows, :] for q in range(19)], kind[rows, :] == 0)
        for q in range(19):
            post1[SLOT[q], z + 1, pl.ds(rb * 8 + PAD, 8), :] = kept[q]
        for i in range(4):
            vel[i, z, pl.ds(rb * 8, 8), :] = velocity[i]

    faces1, gas_copies = [], []
    for third in range(3):
        for rb in range(3 * third, 3 * third + 3):
            part(rb).wait()
        over(lambda j: (lax.div(j, 3), 3 * third + lax.rem(j, 3)), 12, first)
        if third == 0:
            pl.semaphore_wait(barrier, N_GZ - 1 + N_GY - 1 + 4)
        faces1 += send_all(post1, face_moves(third), halo_s, halo_r, 2 * third)
        if third == 0:
            gas_copies += send_all(gas_pad, gas_moves[:2], gas_s, gas_r, 0)
        if third == 1:
            gas_copies += send_all(gas_pad, gas_moves[2:], gas_s, gas_r, 2)
    sides1 = send_all(post1, side_moves, halo_s, halo_r, 6)
    corners1 = send_all(post1, corner_moves, halo_s, halo_r, 10)

    for copy in small:
        copy.wait()
    row, lane = tile_iota(0, (DEVICES, DEVICES)), tile_iota(1, (DEVICES, DEVICES))
    holder = lane == (row & (N_GZ - 1)) * N_GY + (row >> 5)
    rows_of = jnp.zeros((DEVICES, DEVICES), jnp.float32)
    for s in range(CAP):
        asked = want[s : s + 1, :].astype(jnp.float32)
        column = jnp.sum(jnp.where(holder, asked, 0.0), axis=1, keepdims=True)
        rows_of = jnp.where(lane == s, column, rows_of)
    ask_send[...] = rows_of.reshape(N_GY, N_GZ, DEVICES)
    ask_mid[gy] = ask_send[gy]
    for i in range(1, N_GY):
        peer = lax.rem(gy + i, N_GY)
        pltpu.make_async_remote_copy(
            src_ref=ask_send.at[peer],
            dst_ref=ask_mid.at[gy],
            send_sem=all_s.at[0],
            recv_sem=all_r.at[0],
            device_id=(gz, peer),
            device_id_type=MESH,
        ).start()

    def ask_columns():
        pltpu.make_async_copy(
            ask_send.at[: N_GY - 1], ask_mid.at[: N_GY - 1], all_r.at[0]
        ).wait()
        ask_recv[:, pl.ds(gz, 1), :] = ask_mid[:, pl.ds(gz, 1), :]

        def ask(i, carry):
            peer = lax.rem(gz + i, N_GZ)
            pltpu.make_async_remote_copy(
                src_ref=ask_mid.at[:, pl.ds(peer, 1)],
                dst_ref=ask_recv.at[:, pl.ds(gz, 1)],
                send_sem=all_s.at[3],
                recv_sem=all_r.at[3],
                device_id=(peer, gy),
                device_id_type=MESH,
            ).start()
            return carry

        lax.fori_loop(1, N_GZ, ask, 0, unroll=N_GZ - 1)

    def masks(z, rb):
        place_x = lax.rem(
            (rb * 8 + tile_iota(0)) * 128 + tile_iota(1), jnp.full((8, 128), ACROSS, jnp.int32)
        )
        left, right = place_x == 0, place_x == ACROSS - 1
        own = gas_pad[z + 1, pl.ds(rb * 8 + PAD, 8), :]
        bits = own
        for q in range(1, 19):
            step_x, step_y, step_z = DIRS[q]
            source = shifted(window(gas_pad, (), z + 1 - step_z, rb), step_x, step_y, left, right)
            bits = bits | (jnp.maximum(source, own) << q)
        bits = bits | (left.astype(jnp.int32) << LEFT_BIT) | (right.astype(jnp.int32) << RIGHT_BIT)
        mask[z, pl.ds(rb * 8, 8), :] = bits

    def second(z, rb):
        new, gas = passed(post1, mask, vel, z, rb)
        kept, velocity = collide(new, gas)
        for q in range(19):
            post2[SLOT[q], z + 1, pl.ds(rb * 8 + PAD, 8), :] = kept[q]
        for i in range(4):
            vel[i, z, pl.ds(rb * 8, 8), :] = velocity[i]

    over(inner_tile, 14, masks, 7)
    over(inner_tile, 14, second, 7)
    ask_columns()
    for copy in gas_copies:
        copy.wait()
    over(side_tile, 4, masks)
    for third in range(3):
        over(face_tile(third), 6, masks)
    for copy in sides1:
        copy.wait()
    over(side_tile, 4, second)
    for copy in faces1 + corners1:
        copy.wait()
    faces2 = []
    for third in range(3):
        over(face_tile(third), 6, second)
        faces2 += send_all(post2, face_moves(third), halo_s, halo_r, 14 + 2 * third)
    corners2 = send_all(post2, corner_moves, halo_s, halo_r, 24)
    sides2 = send_all(post2, side_moves, halo_s, halo_r, 20)

    big0, big1 = tile_iota(0, (SLOTS, SLOTS)), tile_iota(1, (SLOTS, SLOTS))
    diagonal = big0 == big1
    spot = place[...]
    spot = (spot & 3) * DEVICES + ((spot >> 2) & 3) * N_GZ + (spot >> 4)
    slot_hot[...] = (big0 == spot).astype(jnp.float32).astype(jnp.bfloat16)
    spot_col = jnp.sum(
        jnp.where(diagonal, spot.astype(jnp.float32), 0.0), axis=1, keepdims=True
    )
    ray_hot[...] = (big1.astype(jnp.float32) == spot_col).astype(jnp.float32).astype(jnp.bfloat16)
    eye_rays = tile_iota(0, (RAYS, RAYS)) == tile_iota(1, (RAYS, RAYS))
    live[...] = jnp.broadcast_to(
        jnp.sum(jnp.where(eye_rays, hits[...].astype(jnp.float32), 0.0), axis=1, keepdims=True),
        (RAYS, 128),
    )
    others = ask_recv.at[:, : N_GZ - 1]
    pltpu.make_async_copy(others, others, all_r.at[3]).wait()
    asked_rows = ask_recv[...].reshape(DEVICES, DEVICES)
    block = tile_iota(1, (DEVICES, NB_DEV)).astype(jnp.float32)
    lines = line[...].astype(jnp.float32)
    wanted_row = []
    for s in range(CAP):
        chosen = asked_rows[:, s : s + 1] == block
        wanted_row.append(jnp.sum(jnp.where(chosen, lines, 0.0), axis=1, keepdims=True))
    row_col = jnp.concatenate(wanted_row, axis=0)
    cell_hot[...] = (
        (tile_iota(1, (SLOTS, 384)).astype(jnp.float32) == row_col)
        .astype(jnp.float32)
        .astype(jnp.bfloat16)
    )
    row_row = jnp.sum(jnp.where(diagonal, row_col, 0.0), axis=0, keepdims=True)
    back_hot[...] = (
        (tile_iota(0, (CELL_ROWS, SLOTS)).astype(jnp.float32) == row_row)
        .astype(jnp.float32)
        .astype(jnp.bfloat16)
    )
    cells[CELL_ROWS:, :] = jnp.zeros((384 - CELL_ROWS, 128), jnp.float32)

    def last(z, rb):
        new, gas = passed(post2, mask, vel, z, rb)
        rows = pl.ds(rb * 32 + z, 8, stride=DEPTH)
        for q in range(19):
            field[q, rows, :] = new[q]
        density, ux, uy, uz = moments(new)
        for i, v in enumerate((ux, uy, uz)):
            vel[i, z, pl.ds(rb * 8, 8), :] = v
        cosine = 0.2 + 0.7 / (1.0 + jnp.exp(-8.0 * (density - 1.0)))
        index = 1.0 + temp[rows, :]
        upper = (index - cosine) * (index - cosine) + 1.0
        lower = (index + cosine) * (index + cosine) + 1.0
        cells[pl.ds(pl.multiple_of(z * ROWS + rb * 8, 8), 8), :] = jnp.where(
            gas, 1.0, upper / lower
        )

    over(inner_tile, 14, last, 7)
    for copy in sides2:
        copy.wait()
    over(side_tile, 4, last)
    for copy in faces2 + corners2:
        copy.wait()
    for third in range(3):
        over(face_tile(third), 6, last)

    place_x, place_y = lax.div(gz, 8), lax.rem(lax.div(gz, 2), 4)
    core = lax.rem(gz, 2)
    x_on = [lax.rem(place_x + i, 4) * 8 for i in range(4)]
    y_on = [lax.rem(place_y + i, 4) * 2 for i in range(4)]
    cores = (core, 1 - core)
    me = gy * N_GZ + gz

    def onward(own, k):
        return lax.rem(own + 10 - lax.div(k * (k + 1), 2), 4)

    def to_all(src, dst, n):
        dst[:, pl.ds(me, 1), :] = src[:, pl.ds(me, 1), :]

        def to_one(column, z):
            pltpu.make_async_remote_copy(
                src_ref=src.at[:, pl.ds(z * N_GZ + column, 1)],
                dst_ref=dst.at[:, pl.ds(me, 1)],
                send_sem=all_s.at[n],
                recv_sem=all_r.at[n],
                device_id=(column, z),
                device_id_type=MESH,
            ).start()

        def to_eight(i, carry):
            x = onward(place_x, lax.div(i, 4)) * 8
            z = onward(gy, lax.rem(i, 4))
            for y in (2, 1, 3, 0):
                for other in (1, 0):
                    to_one(x + y_on[y] + cores[other], z)
            return carry

        lax.fori_loop(0, 15, to_eight, 0)
        for y in (2, 1, 3, 0):
            for other in (1, 0):
                if (y, other) != (0, 0):
                    to_one(x_on[0] + y_on[y] + cores[other], gy)
        pltpu.make_async_copy(
            src.at[:, pl.ds(0, DEVICES - 1)], dst.at[:, pl.ds(0, DEVICES - 1)], all_r.at[n]
        ).wait()

    row_send[...] = pick(cell_hot[...], cells[...]).reshape(CAP, DEVICES, 128)
    to_all(row_send, row_recv, 1)

    ray_rows[...] = pick(ray_hot[...], row_recv[...].reshape(SLOTS, 128))
    energy = beam[...]
    hit_count = live[...]
    for j in range(BOUNCES):
        at = pl.ds(j, RAYS, stride=BOUNCES)
        ratio = ray_rows[at, :]
        ray_rows[at, :] = jnp.where(hit_count > float(j), energy * (1.0 - ratio), 0.0)
        energy = energy * ratio
    heat_send[...] = pick(slot_hot[...], ray_rows[...]).reshape(CAP, DEVICES, 128)
    to_all(heat_send, heat_recv, 2)

    cells[pl.ds(0, CELL_ROWS), :] = pick(back_hot[...], heat_recv[...].reshape(SLOTS, 128))

    def sources(z, rb):
        at = pl.ds(pl.multiple_of(z * ROWS + rb * 8, 8), 8)
        source = temp[pl.ds(rb * 32 + z, 8, stride=DEPTH), :] + cells[at, :]
        eighth = 0.125 * source
        for i in range(3):
            moved = eighth * (4.0 * vel[i, z, pl.ds(rb * 8, 8), :])
            thermal[2 * i, z + 1, pl.ds(rb * 8 + PAD, 8), :] = eighth + moved
            thermal[2 * i + 1, z + 1, pl.ds(rb * 8 + PAD, 8), :] = eighth - moved
        cells[at, :] = 0.25 * source

    over(any_tile, 36, sources, 12)
    th_moves = (
        ((4, 4, body), (4, 0, body), (up, gy)),
        ((5, 1, body), (5, 5, body), (down, gy)),
        ((2, planes, high_src), (2, planes, high_dst), (gz, north)),
        ((3, planes, low_src), (3, planes, low_dst), (gz, south)),
    )
    for copy in send_all(thermal, th_moves, th_s, th_r, 0):
        copy.wait()
    pltpu.make_async_copy(
        ask_send.at[: N_GY - 1], ask_mid.at[: N_GY - 1], all_s.at[0]
    ).wait()
    pltpu.make_async_copy(others, others, all_s.at[3]).wait()
    for n, ref in ((1, row_send), (2, heat_send)):
        done = ref.at[:, pl.ds(0, DEVICES - 1)]
        pltpu.make_async_copy(done, done, all_s.at[n]).wait()


def finish(field, thermal, cells, out_hbm, temp_out_hbm, temp_out, out_sem, temp_sem):
    copies = []
    for i, (lo, hi) in enumerate(((0, 5), (5, 10), (10, 15), (15, 19))):
        copy = pltpu.make_async_copy(field.at[lo:hi], out_hbm.at[lo:hi], out_sem.at[i])
        copy.start()
        copies.append(copy)

    def gather(z, rb):
        place_x = lax.rem(
            (rb * 8 + tile_iota(0)) * 128 + tile_iota(1), jnp.full((8, 128), ACROSS, jnp.int32)
        )
        left, right = place_x == 0, place_x == ACROSS - 1
        total = cells[pl.ds(pl.multiple_of(z * ROWS + rb * 8, 8), 8), :]
        for i in range(6):
            step_x, step_y, step_z = DIRS[i + 1]
            total = total + shifted(
                window(thermal, (i,), z + 1 - step_z, rb), step_x, step_y, left, right
            )
        temp_out[pl.ds(rb * 32 + z, 8, stride=DEPTH), :] = total

    over(lambda j: (lax.rem(j, 4), lax.div(j, 4)), 36, gather, 12)
    copy = pltpu.make_async_copy(temp_out, temp_out_hbm, temp_sem)
    copy.start()
    copy.wait()
    for copy in copies:
        copy.wait()


def fold(x):
    lead = x.shape[:-2]
    n = len(lead)
    x = x.reshape(lead + (DEPTH, ROWS, 128)).transpose(tuple(range(n)) + (n + 1, n, n + 2))
    return x.reshape(lead + (CELL_ROWS, 128))


def unfold(x):
    lead = x.shape[:-2]
    n = len(lead)
    x = x.reshape(lead + (ROWS, DEPTH, 128)).transpose(tuple(range(n)) + (n + 1, n, n + 2))
    return x.reshape(lead + (DEPTH, ROWS * 128))


def per_device(populations, kinds, temperature, lines, wanted, places, hits, beam):
    f32, i32, bf16 = jnp.float32, jnp.int32, jnp.bfloat16
    dma = pltpu.SemaphoreType.DMA
    vmem = pl.BlockSpec(memory_space=pltpu.VMEM)
    whole = pl.BlockSpec(memory_space=pl.ANY)
    operands = (
        fold(populations),
        fold(kinds),
        fold(temperature),
        lines,
        wanted[0].T,
        places,
        hits,
        beam[0],
    )
    field, thermal, cells = pl.pallas_call(
        kernel,
        out_shape=(
            pltpu.VMEM((19, CELL_ROWS, 128), f32),
            pltpu.VMEM((6, DEPTH + 2, PLANE, 128), f32),
            pltpu.VMEM((384, 128), f32),
        ),
        in_specs=[whole] * 8,
        out_specs=[vmem] * 3,
        scratch_shapes=[
            pltpu.VMEM((19, CELL_ROWS, 128), f32),
            pltpu.VMEM((CELL_ROWS, 128), i32),
            pltpu.VMEM((CELL_ROWS, 128), f32),
            pltpu.VMEM((1, NB_DEV), i32),
            pltpu.VMEM((CAP, DEVICES), i32),
            pltpu.VMEM((1, SLOTS), i32),
            pltpu.VMEM((1, RAYS), i32),
            pltpu.VMEM((RAYS, 128), f32),
            pltpu.VMEM((DEPTH + 2, PLANE, 128), i32),
            pltpu.VMEM((19, DEPTH + 2, PLANE, 128), f32),
            pltpu.VMEM((19, DEPTH + 2, PLANE, 128), f32),
            pltpu.VMEM((DEPTH, ROWS, 128), i32),
            pltpu.VMEM((4, DEPTH, ROWS, 128), f32),
            pltpu.VMEM((N_GY, N_GZ, 128), f32),
            pltpu.VMEM((N_GY, N_GZ, 128), f32),
            pltpu.VMEM((N_GY, N_GZ, 128), f32),
            pltpu.VMEM((CAP, DEVICES, 128), f32),
            pltpu.VMEM((CAP, DEVICES, 128), f32),
            pltpu.VMEM((CAP, DEVICES, 128), f32),
            pltpu.VMEM((CAP, DEVICES, 128), f32),
            pltpu.VMEM((SLOTS, SLOTS), bf16),
            pltpu.VMEM((SLOTS, SLOTS), bf16),
            pltpu.VMEM((SLOTS, 384), bf16),
            pltpu.VMEM((CELL_ROWS, SLOTS), bf16),
            pltpu.VMEM((SLOTS, 128), f32),
            pltpu.VMEM((RAYS, 128), f32),
            dma((9,)),
            dma((7,)),
            dma((8,)),
            dma((8,)),
            dma((28,)),
            dma((28,)),
            dma((4,)),
            dma((4,)),
            dma((4,)),
            dma((4,)),
        ],
        compiler_params=pltpu.CompilerParams(
            collective_id=0, has_side_effects=True, vmem_limit_bytes=40 * 2**20
        ),
        cost_estimate=pl.CostEstimate(
            flops=100_000_000, bytes_accessed=7_000_000, transcendentals=40_000
        ),
    )(*[pltpu.with_memory_space_constraint(x, pltpu.HBM) for x in operands])
    lattice, heated = pl.pallas_call(
        finish,
        out_shape=(
            jax.ShapeDtypeStruct((19, CELL_ROWS, 128), f32),
            jax.ShapeDtypeStruct((CELL_ROWS, 128), f32),
        ),
        in_specs=[vmem] * 3,
        out_specs=[whole] * 2,
        scratch_shapes=[pltpu.VMEM((CELL_ROWS, 128), f32), dma((4,)), dma],
        compiler_params=pltpu.CompilerParams(vmem_limit_bytes=40 * 2**20),
        cost_estimate=pl.CostEstimate(
            flops=1_000_000, bytes_accessed=7_000_000, transcendentals=0
        ),
    )(*[pltpu.with_memory_space_constraint(x, pltpu.VMEM) for x in (field, thermal, cells)])
    return unfold(lattice), unfold(heated)


def solution(mesh):
    placed = (
        P(None, "gz", "gy"),
        P("gz", "gy"),
        P("gz", "gy"),
        P(("gz", "gy"), None),
        P(("gz", "gy"), None, None),
        P(("gz", "gy"), None),
        P(("gz", "gy"), None),
        P(("gz", "gy"), None, None),
    )
    return jax.shard_map(
        per_device,
        mesh=mesh,
        in_specs=placed,
        out_specs=(P(None, "gz", "gy"), P("gz", "gy")),
        check_vma=False,
    )
```

```python
import jax
import jax.numpy as jnp
from jax import lax
from jax.experimental import pallas as pl
from jax.experimental.pallas import tpu as pltpu
from jax.sharding import PartitionSpec as P

MESH = pl.DeviceIdType.MESH
N_GZ = 32
N_GY = 4
DEVICES = 128
CAP = 4
SLOTS = 512
NB_DEV = 64
RAYS = 64
BOUNCES = 8
ACROSS = 192
DEPTH = 4
ROWS = 72
CELL_ROWS = 288
PAD = 8
PLANE = ROWS + 2 * PAD

DIRS = [
    (0, 0, 0),
    (1, 0, 0),
    (-1, 0, 0),
    (0, 1, 0),
    (0, -1, 0),
    (0, 0, 1),
    (0, 0, -1),
    (1, 1, 0),
    (-1, -1, 0),
    (1, -1, 0),
    (-1, 1, 0),
    (1, 0, 1),
    (-1, 0, -1),
    (1, 0, -1),
    (-1, 0, 1),
    (0, 1, 1),
    (0, -1, -1),
    (0, 1, -1),
    (0, -1, 1),
]
WEIGHTS = [1.0 / 3.0] + [1.0 / 18.0] * 6 + [1.0 / 36.0] * 12
PAIRS = [(q, q + 1) for q in range(1, 19, 2)]
OPP = [0, 2, 1, 4, 3, 6, 5, 8, 7, 10, 9, 12, 11, 14, 13, 16, 15, 18, 17]
RELAX = 0.8
THIRDS = (0, 2, 1)
ORDER = [18, 5, 11, 14, 15, 17, 12, 13, 6, 16, 4, 8, 9, 1, 2, 0, 3, 7, 10]
SLOT = [ORDER.index(q) for q in range(19)]
LEFT_BIT = 19
RIGHT_BIT = 20


def tile_iota(axis, shape=(8, 128)):
    return lax.broadcasted_iota(jnp.int32, shape, axis)


def moments(f):
    d = {a: f[a] - f[b] for a, b in PAIRS}
    s = {a: f[a] + f[b] for a, b in PAIRS}
    density = (
        ((s[1] + s[3]) + (s[5] + s[7])) + ((s[9] + s[11]) + (s[13] + s[15])) + (s[17] + f[0])
    )
    mx = (d[1] + d[7]) + (d[9] + d[11]) + d[13]
    my = (d[3] + d[7]) + (d[15] - d[9]) + d[17]
    mz = (d[5] + d[11]) + (d[15] - d[13]) - d[17]
    inv = 1.0 / density
    return density, mx * inv, my * inv, mz * inv


def along(u, q):
    total = None
    for step, part in zip(DIRS[q], u):
        if step == 0:
            continue
        if total is None:
            total = part if step > 0 else -part
        else:
            total = total + part if step > 0 else total - part
    return total


def collide(f, gas):
    density, ux, uy, uz = moments(f)
    base = 1.0 - 1.5 * (ux * ux + uy * uy + uz * uz)
    triple = (3.0 * ux, 3.0 * uy, 3.0 * uz)
    kept = [None] * 19
    keep = 1.0 - RELAX
    scaled = {w: (RELAX * w) * density for w in (1.0 / 18.0, 1.0 / 36.0)}
    post = keep * f[0] + (RELAX / 3.0) * density * base
    kept[0] = jnp.where(gas, -f[0], post)
    for a, b in PAIRS:
        wd = scaled[WEIGHTS[a]]
        c = along(triple, a)
        even = wd * (base + 0.5 * (c * c))
        odd = wd * c
        kept[a] = jnp.where(gas, -f[b], keep * f[a] + (even + odd))
        kept[b] = jnp.where(gas, -f[a], keep * f[b] + (even - odd))
    zero = jnp.zeros_like(ux)
    velocity = [jnp.where(gas, zero, v) for v in (ux, uy, uz, base)]
    return kept, velocity


def shifted(load, step_x, step_y, left, right):
    lane = tile_iota(1)

    def flat(by):
        rows, lanes = by // 128, by % 128
        if lanes == 0:
            return load(-rows)
        picked = jnp.where(lane >= 128 - lanes, load(-rows - 1), load(-rows))
        return pltpu.roll(picked, lanes, 1)

    main = flat(step_x + ACROSS * step_y)
    if step_x == 0:
        return main
    by = step_x + ACROSS * step_y - ACROSS * step_x
    rows, lanes = by // 128, by % 128
    targets = (0, 64) if step_x == 1 else (63, 127)
    if all(t < lanes for t in targets):
        wrapped = pltpu.roll(load(-rows - 1), lanes, 1)
    elif all(t >= lanes for t in targets):
        wrapped = pltpu.roll(load(-rows), lanes, 1)
    else:
        wrapped = flat(by)
    return jnp.where(left if step_x == 1 else right, wrapped, main)


def window(ref, lead, z, rb):
    def load(n):
        return ref[(*lead, z, pl.ds(rb * 8 + (PAD + n), 8), slice(None))]

    return load


def passed(post_ref, mask_ref, vel_ref, z, rb):
    mask = mask_ref[z, pl.ds(rb * 8, 8), :]
    left = (mask & (1 << LEFT_BIT)) != 0
    right = (mask & (1 << RIGHT_BIT)) != 0
    ux, uy, uz, base = [vel_ref[i, z, pl.ds(rb * 8, 8), :] for i in range(4)]
    centre = [post_ref[SLOT[q], z + 1, pl.ds(rb * 8 + PAD, 8), :] for q in range(19)]
    new = [None] * 19
    new[0] = jnp.where((mask & 1) != 0, -centre[0], centre[0])
    triple = (3.0 * ux, 3.0 * uy, 3.0 * uz)
    for a, b in PAIRS:
        c = along(triple, a)
        both = (2.0 * WEIGHTS[a]) * (base + 0.5 * (c * c))
        for q, back in ((a, b), (b, a)):
            step_x, step_y, step_z = DIRS[q]
            source = shifted(
                window(post_ref, (SLOT[q],), z + 1 - step_z, rb), step_x, step_y, left, right
            )
            new[q] = jnp.where((mask & (1 << q)) != 0, both - centre[back], source)
    return new, (mask & 1) != 0


def two_terms(x):
    high = x.astype(jnp.bfloat16)
    low = (x - high.astype(jnp.float32)).astype(jnp.bfloat16)
    return jnp.concatenate([high, low], axis=1)


def pick(one_hot, values):
    both = jnp.dot(one_hot, two_terms(values), preferred_element_type=jnp.float32)
    return both[:, :128] + both[:, 128:]


def inner_tile(j):
    return 1 + lax.div(j, 7), 1 + lax.rem(j, 7)


def side_tile(j):
    return 1 + lax.div(j, 2), lax.rem(j, 2) * 8


def face_tile(first_rb, count):
    return lambda j: (lax.div(j, count) * 3, first_rb + lax.rem(j, count))


def any_tile(j):
    return lax.div(j, 9), lax.rem(j, 9)


def over(tile, count, body, unroll=None):
    def step(j, carry):
        body(*tile(j))
        return carry

    lax.fori_loop(0, count, step, 0, unroll=unroll or count)


def kernel(
    pop_hbm,
    kind_hbm,
    temp_hbm,
    line_hbm,
    want_hbm,
    place_hbm,
    hits_hbm,
    beam_hbm,
    field,
    thermal,
    cells,
    inputs,
    kind,
    temp,
    line,
    want,
    place,
    hits,
    beam,
    gas_pad,
    post1,
    post2,
    mask,
    vel,
    ask_send,
    ask_mid,
    ask_recv,
    row_send,
    row_recv,
    heat_send,
    heat_recv,
    slot_hot,
    ray_hot,
    cell_hot,
    back_hot,
    ray_rows,
    live,
    load_sem,
    small_sem,
    gas_s,
    gas_r,
    halo_s,
    halo_r,
    all_s,
    all_r,
    th_s,
    th_r,
):
    gz = lax.axis_index("gz")
    gy = lax.axis_index("gy")
    up, down = lax.rem(gz + 1, N_GZ), lax.rem(gz + N_GZ - 1, N_GZ)
    north, south = lax.rem(gy + 1, N_GY), lax.rem(gy + N_GY - 1, N_GY)

    barrier = pltpu.get_barrier_semaphore()

    def greet(i, carry):
        pl.semaphore_signal(
            barrier, 1, device_id=(lax.rem(gz + i, N_GZ), gy), device_id_type=MESH
        )
        return carry

    lax.fori_loop(1, N_GZ, greet, 0, unroll=N_GZ - 1)
    for i in range(1, N_GY):
        pl.semaphore_signal(barrier, 1, device_id=(gz, lax.rem(gy + i, N_GY)), device_id_type=MESH)
    for peer in ((up, north), (up, south), (down, north), (down, south)):
        pl.semaphore_signal(barrier, 1, device_id=peer, device_id_type=MESH)

    kind_copy = pltpu.make_async_copy(kind_hbm, kind, small_sem.at[6])
    kind_copy.start()
    want_copy = pltpu.make_async_copy(want_hbm, want, small_sem.at[5])
    want_copy.start()

    def part(rb):
        rows = pl.ds(rb * 32, 32)
        return pltpu.make_async_copy(pop_hbm.at[:, rows], inputs.at[:, rows], load_sem.at[rb])

    for third in THIRDS:
        for rb in range(3 * third, 3 * third + 3):
            part(rb).start()

    small = []
    for i, (src, dst) in enumerate(
        (
            (line_hbm, line),
            (place_hbm, place),
            (hits_hbm, hits),
            (beam_hbm, beam),
            (temp_hbm, temp),
        )
    ):
        copy = pltpu.make_async_copy(src, dst, small_sem.at[i])
        copy.start()
        small.append(copy)

    kind_copy.wait()

    def flags(z, rb):
        gas = kind[pl.ds(rb * 32 + z, 8, stride=DEPTH), :] == 0
        gas_pad[z + 1, pl.ds(rb * 8 + PAD, 8), :] = gas.astype(jnp.int32)

    over(any_tile, 36, flags, 12)

    want_copy.wait()
    row, lane = tile_iota(0, (DEVICES, DEVICES)), tile_iota(1, (DEVICES, DEVICES))
    holder = lane == (row & (N_GZ - 1)) * N_GY + (row >> 5)
    rows_of = jnp.zeros((DEVICES, DEVICES), jnp.float32)
    for s in range(CAP):
        asked = want[s : s + 1, :].astype(jnp.float32)
        column = jnp.sum(jnp.where(holder, asked, 0.0), axis=1, keepdims=True)
        rows_of = jnp.where(lane == s, column, rows_of)
    ask_send[...] = rows_of.reshape(N_GY, N_GZ, DEVICES)
    ask_mid[gy] = ask_send[gy]

    low_src, low_dst = slice(PAD, PAD + 2), slice(PAD + ROWS, PAD + ROWS + 2)
    high_src, high_dst = slice(PAD + ROWS - 2, PAD + ROWS), slice(PAD - 2, PAD)
    body = slice(PAD, PAD + ROWS)
    planes = slice(1, 1 + DEPTH)

    def send(ref, src, dst, s, r, peer):
        copy = pltpu.make_async_remote_copy(
            src_ref=ref.at[src],
            dst_ref=ref.at[dst],
            send_sem=s,
            recv_sem=r,
            device_id=peer,
            device_id_type=MESH,
        )
        copy.start()
        return copy

    def face_moves(first_rb, count):
        rows = slice(PAD + 8 * first_rb, PAD + 8 * (first_rb + count))
        return (
            ((slice(0, 5), 4, rows), (slice(0, 5), 0, rows), (up, gy)),
            ((slice(5, 10), 1, rows), (slice(5, 10), 5, rows), (down, gy)),
        )

    side_moves = (
        ((slice(4, 6), planes, high_src), (slice(4, 6), planes, high_dst), (gz, north)),
        ((slice(16, 19), planes, high_src), (slice(16, 19), planes, high_dst), (gz, north)),
        ((slice(9, 13), planes, low_src), (slice(9, 13), planes, low_dst), (gz, south)),
        ((slice(0, 1), planes, low_src), (slice(0, 1), planes, low_dst), (gz, south)),
    )
    corner_moves = (
        ((4, 4, high_src), (4, 0, high_dst), (up, north)),
        ((9, 1, low_src), (9, 5, low_dst), (down, south)),
        ((5, 1, high_src), (5, 5, high_dst), (down, north)),
        ((0, 4, low_src), (0, 0, low_dst), (up, south)),
    )

    def send_all(ref, moves, s, r, first_sem):
        return [
            send(ref, src, dst, s.at[first_sem + i], r.at[first_sem + i], peer)
            for i, (src, dst, peer) in enumerate(moves)
        ]

    gas_moves = (
        ((4, body), (0, body), (up, gy)),
        ((1, body), (5, body), (down, gy)),
        ((planes, high_src), (planes, high_dst), (gz, north)),
        ((planes, low_src), (planes, low_dst), (gz, south)),
        ((4, high_src), (0, high_dst), (up, north)),
        ((4, low_src), (0, low_dst), (up, south)),
        ((1, high_src), (5, high_dst), (down, north)),
        ((1, low_src), (5, low_dst), (down, south)),
    )

    def first(z, rb):
        rows = pl.ds(rb * 32 + z, 8, stride=DEPTH)
        kept, velocity = collide([inputs[q, rows, :] for q in range(19)], kind[rows, :] == 0)
        for q in range(19):
            post1[SLOT[q], z + 1, pl.ds(rb * 8 + PAD, 8), :] = kept[q]
        for i in range(4):
            vel[i, z, pl.ds(rb * 8, 8), :] = velocity[i]

    def ask_row():
        for i in range(1, N_GY):
            peer = lax.rem(gy + i, N_GY)
            pltpu.make_async_remote_copy(
                src_ref=ask_send.at[peer],
                dst_ref=ask_mid.at[gy],
                send_sem=all_s.at[0],
                recv_sem=all_r.at[0],
                device_id=(gz, peer),
                device_id_type=MESH,
            ).start()

    pl.semaphore_wait(barrier, N_GZ - 1 + N_GY - 1 + 4)
    gas_copies = send_all(gas_pad, gas_moves, gas_s, gas_r, 0)
    ask_row()
    faces1 = []
    for third in THIRDS:
        for rb in range(3 * third, 3 * third + 3):
            part(rb).wait()
        over(lambda j: (lax.div(j, 3), 3 * third + lax.rem(j, 3)), 12, first)
        faces1.append(send_all(post1, face_moves(3 * third, 3), halo_s, halo_r, 2 * third))
        if third == THIRDS[1]:
            corners1 = send_all(post1, corner_moves, halo_s, halo_r, 10)
            sides1 = send_all(post1, side_moves, halo_s, halo_r, 6)
    for copy in small:
        copy.wait()

    def ask_columns():
        pltpu.make_async_copy(
            ask_send.at[: N_GY - 1], ask_mid.at[: N_GY - 1], all_r.at[0]
        ).wait()
        ask_recv[:, pl.ds(gz, 1), :] = ask_mid[:, pl.ds(gz, 1), :]

        def ask(i, carry):
            peer = lax.rem(gz + i, N_GZ)
            pltpu.make_async_remote_copy(
                src_ref=ask_mid.at[:, pl.ds(peer, 1)],
                dst_ref=ask_recv.at[:, pl.ds(gz, 1)],
                send_sem=all_s.at[3],
                recv_sem=all_r.at[3],
                device_id=(peer, gy),
                device_id_type=MESH,
            ).start()
            return carry

        lax.fori_loop(1, N_GZ, ask, 0, unroll=N_GZ - 1)

    def masks(z, rb):
        place_x = lax.rem(
            (rb * 8 + tile_iota(0)) * 128 + tile_iota(1), jnp.full((8, 128), ACROSS, jnp.int32)
        )
        left, right = place_x == 0, place_x == ACROSS - 1
        own = gas_pad[z + 1, pl.ds(rb * 8 + PAD, 8), :]
        bits = own
        for q in range(1, 19):
            step_x, step_y, step_z = DIRS[q]
            source = shifted(window(gas_pad, (), z + 1 - step_z, rb), step_x, step_y, left, right)
            bits = bits | (jnp.maximum(source, own) << q)
        bits = bits | (left.astype(jnp.int32) << LEFT_BIT) | (right.astype(jnp.int32) << RIGHT_BIT)
        mask[z, pl.ds(rb * 8, 8), :] = bits

    def second(z, rb):
        new, gas = passed(post1, mask, vel, z, rb)
        kept, velocity = collide(new, gas)
        for q in range(19):
            post2[SLOT[q], z + 1, pl.ds(rb * 8 + PAD, 8), :] = kept[q]
        for i in range(4):
            vel[i, z, pl.ds(rb * 8, 8), :] = velocity[i]

    over(inner_tile, 14, masks, 7)
    over(inner_tile, 14, second, 7)
    ask_columns()
    for copy in gas_copies:
        copy.wait()
    over(side_tile, 4, masks)
    over(face_tile(0, 9), 18, masks, 9)
    for copy in sides1:
        copy.wait()
    over(side_tile, 4, second)
    faces2 = []

    def second_faces(first_rb, count):
        over(face_tile(first_rb, count), 2 * count, second)

    def send_faces(first_rb, count):
        faces2.append(
            send_all(post2, face_moves(first_rb, count), halo_s, halo_r, 14 + 2 * len(faces2))
        )

    for copy in faces1[0]:
        copy.wait()
    second_faces(1, 1)
    for copy in faces1[1]:
        copy.wait()
    second_faces(7, 1)
    for copy in corners1:
        copy.wait()
    second_faces(0, 1)
    send_faces(0, 2)
    second_faces(8, 1)
    send_faces(7, 2)
    corners2 = send_all(post2, corner_moves, halo_s, halo_r, 26)
    sides2 = send_all(post2, side_moves, halo_s, halo_r, 22)
    for copy in faces1[2]:
        copy.wait()
    second_faces(2, 3)
    send_faces(2, 3)
    second_faces(5, 2)
    send_faces(5, 2)

    big0, big1 = tile_iota(0, (SLOTS, SLOTS)), tile_iota(1, (SLOTS, SLOTS))
    diagonal = big0 == big1
    spot = place[...]
    spot = (spot & 3) * DEVICES + ((spot >> 2) & 3) * N_GZ + (spot >> 4)
    slot_hot[...] = (big0 == spot).astype(jnp.float32).astype(jnp.bfloat16)
    spot_col = jnp.sum(
        jnp.where(diagonal, spot.astype(jnp.float32), 0.0), axis=1, keepdims=True
    )
    ray_hot[...] = (big1.astype(jnp.float32) == spot_col).astype(jnp.float32).astype(jnp.bfloat16)
    eye_rays = tile_iota(0, (RAYS, RAYS)) == tile_iota(1, (RAYS, RAYS))
    live[...] = jnp.broadcast_to(
        jnp.sum(jnp.where(eye_rays, hits[...].astype(jnp.float32), 0.0), axis=1, keepdims=True),
        (RAYS, 128),
    )
    others = ask_recv.at[:, : N_GZ - 1]
    pltpu.make_async_copy(others, others, all_r.at[3]).wait()
    asked_rows = ask_recv[...].reshape(DEVICES, DEVICES)
    block = tile_iota(1, (DEVICES, NB_DEV)).astype(jnp.float32)
    lines = line[...].astype(jnp.float32)
    wanted_row = []
    for s in range(CAP):
        chosen = asked_rows[:, s : s + 1] == block
        wanted_row.append(jnp.sum(jnp.where(chosen, lines, 0.0), axis=1, keepdims=True))
    row_col = jnp.concatenate(wanted_row, axis=0)
    cell_hot[...] = (
        (tile_iota(1, (SLOTS, 384)).astype(jnp.float32) == row_col)
        .astype(jnp.float32)
        .astype(jnp.bfloat16)
    )
    row_row = jnp.sum(jnp.where(diagonal, row_col, 0.0), axis=0, keepdims=True)
    back_hot[...] = (
        (tile_iota(0, (CELL_ROWS, SLOTS)).astype(jnp.float32) == row_row)
        .astype(jnp.float32)
        .astype(jnp.bfloat16)
    )
    cells[CELL_ROWS:, :] = jnp.zeros((384 - CELL_ROWS, 128), jnp.float32)

    def last(z, rb):
        new, gas = passed(post2, mask, vel, z, rb)
        rows = pl.ds(rb * 32 + z, 8, stride=DEPTH)
        for q in range(19):
            field[q, rows, :] = new[q]
        density, ux, uy, uz = moments(new)
        for i, v in enumerate((ux, uy, uz)):
            vel[i, z, pl.ds(rb * 8, 8), :] = v
        cosine = 0.2 + 0.7 / (1.0 + jnp.exp(-8.0 * (density - 1.0)))
        index = 1.0 + temp[rows, :]
        upper = (index - cosine) * (index - cosine) + 1.0
        lower = (index + cosine) * (index + cosine) + 1.0
        cells[pl.ds(pl.multiple_of(z * ROWS + rb * 8, 8), 8), :] = jnp.where(
            gas, 1.0, upper / lower
        )

    over(inner_tile, 14, last, 7)
    for copy in sides2:
        copy.wait()
    over(side_tile, 4, last)
    for copy in faces2[0] + faces2[1] + corners2:
        copy.wait()
    over(face_tile(0, 1), 2, last)
    over(face_tile(8, 1), 2, last)
    for copy in faces2[2]:
        copy.wait()
    over(face_tile(1, 3), 6, last)
    for copy in faces2[3]:
        copy.wait()
    over(face_tile(4, 4), 8, last)

    place_x, place_y = lax.div(gz, 8), lax.rem(lax.div(gz, 2), 4)
    core = lax.rem(gz, 2)
    x_on = [lax.rem(place_x + i, 4) * 8 for i in range(4)]
    y_on = [lax.rem(place_y + i, 4) * 2 for i in range(4)]
    cores = (core, 1 - core)
    me = gy * N_GZ + gz

    def onward(own, k):
        return lax.rem(own + 10 - lax.div(k * (k + 1), 2), 4)

    def to_all(src, dst, n):
        dst[:, pl.ds(me, 1), :] = src[:, pl.ds(me, 1), :]

        def to_one(column, z):
            pltpu.make_async_remote_copy(
                src_ref=src.at[:, pl.ds(z * N_GZ + column, 1)],
                dst_ref=dst.at[:, pl.ds(me, 1)],
                send_sem=all_s.at[n],
                recv_sem=all_r.at[n],
                device_id=(column, z),
                device_id_type=MESH,
            ).start()

        def to_eight(i, carry):
            x = onward(place_x, lax.div(i, 4)) * 8
            z = onward(gy, lax.rem(i, 4))
            for y in (2, 1, 3, 0):
                for other in (1, 0):
                    to_one(x + y_on[y] + cores[other], z)
            return carry

        lax.fori_loop(0, 15, to_eight, 0)
        for y in (2, 1, 3, 0):
            for other in (1, 0):
                if (y, other) != (0, 0):
                    to_one(x_on[0] + y_on[y] + cores[other], gy)
        pltpu.make_async_copy(
            src.at[:, pl.ds(0, DEVICES - 1)], dst.at[:, pl.ds(0, DEVICES - 1)], all_r.at[n]
        ).wait()

    row_send[...] = pick(cell_hot[...], cells[...]).reshape(CAP, DEVICES, 128)
    to_all(row_send, row_recv, 1)

    ray_rows[...] = pick(ray_hot[...], row_recv[...].reshape(SLOTS, 128))
    energy = beam[...]
    hit_count = live[...]
    for j in range(BOUNCES):
        at = pl.ds(j, RAYS, stride=BOUNCES)
        ratio = ray_rows[at, :]
        ray_rows[at, :] = jnp.where(hit_count > float(j), energy * (1.0 - ratio), 0.0)
        energy = energy * ratio
    heat_send[...] = pick(slot_hot[...], ray_rows[...]).reshape(CAP, DEVICES, 128)
    to_all(heat_send, heat_recv, 2)

    cells[pl.ds(0, CELL_ROWS), :] = pick(back_hot[...], heat_recv[...].reshape(SLOTS, 128))

    def sources(z, rb):
        at = pl.ds(pl.multiple_of(z * ROWS + rb * 8, 8), 8)
        source = temp[pl.ds(rb * 32 + z, 8, stride=DEPTH), :] + cells[at, :]
        eighth = 0.125 * source
        for i in range(3):
            moved = eighth * (4.0 * vel[i, z, pl.ds(rb * 8, 8), :])
            thermal[2 * i, z + 1, pl.ds(rb * 8 + PAD, 8), :] = eighth + moved
            thermal[2 * i + 1, z + 1, pl.ds(rb * 8 + PAD, 8), :] = eighth - moved
        cells[at, :] = 0.25 * source

    over(any_tile, 36, sources)
    th_moves = (
        ((4, 4, body), (4, 0, body), (up, gy)),
        ((5, 1, body), (5, 5, body), (down, gy)),
        ((2, planes, high_src), (2, planes, high_dst), (gz, north)),
        ((3, planes, low_src), (3, planes, low_dst), (gz, south)),
    )
    for copy in send_all(thermal, th_moves, th_s, th_r, 0):
        copy.wait()
    pltpu.make_async_copy(
        ask_send.at[: N_GY - 1], ask_mid.at[: N_GY - 1], all_s.at[0]
    ).wait()
    pltpu.make_async_copy(others, others, all_s.at[3]).wait()
    for n, ref in ((1, row_send), (2, heat_send)):
        done = ref.at[:, pl.ds(0, DEVICES - 1)]
        pltpu.make_async_copy(done, done, all_s.at[n]).wait()


def finish(field, thermal, cells, out_hbm, temp_out_hbm, temp_out, out_sem, temp_sem):
    copies = []
    for i, (lo, hi) in enumerate(((0, 5), (5, 10), (10, 15), (15, 19))):
        copy = pltpu.make_async_copy(field.at[lo:hi], out_hbm.at[lo:hi], out_sem.at[i])
        copy.start()
        copies.append(copy)

    def gather(z, rb):
        place_x = lax.rem(
            (rb * 8 + tile_iota(0)) * 128 + tile_iota(1), jnp.full((8, 128), ACROSS, jnp.int32)
        )
        left, right = place_x == 0, place_x == ACROSS - 1
        total = cells[pl.ds(pl.multiple_of(z * ROWS + rb * 8, 8), 8), :]
        for i in range(6):
            step_x, step_y, step_z = DIRS[i + 1]
            total = total + shifted(
                window(thermal, (i,), z + 1 - step_z, rb), step_x, step_y, left, right
            )
        temp_out[pl.ds(rb * 32 + z, 8, stride=DEPTH), :] = total

    over(lambda j: (lax.rem(j, 4), lax.div(j, 4)), 36, gather, 12)
    copy = pltpu.make_async_copy(temp_out, temp_out_hbm, temp_sem)
    copy.start()
    copy.wait()
    for copy in copies:
        copy.wait()


def fold(x):
    lead = x.shape[:-2]
    n = len(lead)
    x = x.reshape(lead + (DEPTH, ROWS, 128)).transpose(tuple(range(n)) + (n + 1, n, n + 2))
    return x.reshape(lead + (CELL_ROWS, 128))


def unfold(x):
    lead = x.shape[:-2]
    n = len(lead)
    x = x.reshape(lead + (ROWS, DEPTH, 128)).transpose(tuple(range(n)) + (n + 1, n, n + 2))
    return x.reshape(lead + (DEPTH, ROWS * 128))


def per_device(populations, kinds, temperature, lines, wanted, places, hits, beam):
    f32, i32, bf16 = jnp.float32, jnp.int32, jnp.bfloat16
    dma = pltpu.SemaphoreType.DMA
    vmem = pl.BlockSpec(memory_space=pltpu.VMEM)
    whole = pl.BlockSpec(memory_space=pl.ANY)
    operands = (
        fold(populations),
        fold(kinds),
        fold(temperature),
        lines,
        wanted[0].T,
        places,
        hits,
        beam[0],
    )
    field, thermal, cells = pl.pallas_call(
        kernel,
        out_shape=(
            pltpu.VMEM((19, CELL_ROWS, 128), f32),
            pltpu.VMEM((6, DEPTH + 2, PLANE, 128), f32),
            pltpu.VMEM((384, 128), f32),
        ),
        in_specs=[whole] * 8,
        out_specs=[vmem] * 3,
        scratch_shapes=[
            pltpu.VMEM((19, CELL_ROWS, 128), f32),
            pltpu.VMEM((CELL_ROWS, 128), i32),
            pltpu.VMEM((CELL_ROWS, 128), f32),
            pltpu.VMEM((1, NB_DEV), i32),
            pltpu.VMEM((CAP, DEVICES), i32),
            pltpu.VMEM((1, SLOTS), i32),
            pltpu.VMEM((1, RAYS), i32),
            pltpu.VMEM((RAYS, 128), f32),
            pltpu.VMEM((DEPTH + 2, PLANE, 128), i32),
            pltpu.VMEM((19, DEPTH + 2, PLANE, 128), f32),
            pltpu.VMEM((19, DEPTH + 2, PLANE, 128), f32),
            pltpu.VMEM((DEPTH, ROWS, 128), i32),
            pltpu.VMEM((4, DEPTH, ROWS, 128), f32),
            pltpu.VMEM((N_GY, N_GZ, 128), f32),
            pltpu.VMEM((N_GY, N_GZ, 128), f32),
            pltpu.VMEM((N_GY, N_GZ, 128), f32),
            pltpu.VMEM((CAP, DEVICES, 128), f32),
            pltpu.VMEM((CAP, DEVICES, 128), f32),
            pltpu.VMEM((CAP, DEVICES, 128), f32),
            pltpu.VMEM((CAP, DEVICES, 128), f32),
            pltpu.VMEM((SLOTS, SLOTS), bf16),
            pltpu.VMEM((SLOTS, SLOTS), bf16),
            pltpu.VMEM((SLOTS, 384), bf16),
            pltpu.VMEM((CELL_ROWS, SLOTS), bf16),
            pltpu.VMEM((SLOTS, 128), f32),
            pltpu.VMEM((RAYS, 128), f32),
            dma((9,)),
            dma((7,)),
            dma((8,)),
            dma((8,)),
            dma((30,)),
            dma((30,)),
            dma((4,)),
            dma((4,)),
            dma((4,)),
            dma((4,)),
        ],
        compiler_params=pltpu.CompilerParams(
            collective_id=0, has_side_effects=True, vmem_limit_bytes=40 * 2**20
        ),
        cost_estimate=pl.CostEstimate(
            flops=100_000_000, bytes_accessed=7_000_000, transcendentals=40_000
        ),
    )(*[pltpu.with_memory_space_constraint(x, pltpu.HBM) for x in operands])
    lattice, heated = pl.pallas_call(
        finish,
        out_shape=(
            jax.ShapeDtypeStruct((19, CELL_ROWS, 128), f32),
            jax.ShapeDtypeStruct((CELL_ROWS, 128), f32),
        ),
        in_specs=[vmem] * 3,
        out_specs=[whole] * 2,
        scratch_shapes=[pltpu.VMEM((CELL_ROWS, 128), f32), dma((4,)), dma],
        compiler_params=pltpu.CompilerParams(vmem_limit_bytes=40 * 2**20),
        cost_estimate=pl.CostEstimate(
            flops=1_000_000, bytes_accessed=7_000_000, transcendentals=0
        ),
    )(*[pltpu.with_memory_space_constraint(x, pltpu.VMEM) for x in (field, thermal, cells)])
    return unfold(lattice), unfold(heated)


def solution(mesh):
    placed = (
        P(None, "gz", "gy"),
        P("gz", "gy"),
        P("gz", "gy"),
        P(("gz", "gy"), None),
        P(("gz", "gy"), None, None),
        P(("gz", "gy"), None),
        P(("gz", "gy"), None),
        P(("gz", "gy"), None, None),
    )
    return jax.shard_map(
        per_device,
        mesh=mesh,
        in_specs=placed,
        out_specs=(P(None, "gz", "gy"), P("gz", "gy")),
        check_vma=False,
    )
```

```python
import jax
import jax.numpy as jnp
from jax import lax
from jax.experimental import pallas as pl
from jax.experimental.pallas import tpu as pltpu
from jax.sharding import PartitionSpec as P

MESH = pl.DeviceIdType.MESH
N_GZ = 32
N_GY = 4
DEVICES = 128
CAP = 4
SLOTS = 512
NB_DEV = 64
RAYS = 64
BOUNCES = 8
ACROSS = 192
DEPTH = 4
ROWS = 72
CELL_ROWS = 288
PAD = 8
PLANE = ROWS + 2 * PAD

DIRS = [
    (0, 0, 0),
    (1, 0, 0),
    (-1, 0, 0),
    (0, 1, 0),
    (0, -1, 0),
    (0, 0, 1),
    (0, 0, -1),
    (1, 1, 0),
    (-1, -1, 0),
    (1, -1, 0),
    (-1, 1, 0),
    (1, 0, 1),
    (-1, 0, -1),
    (1, 0, -1),
    (-1, 0, 1),
    (0, 1, 1),
    (0, -1, -1),
    (0, 1, -1),
    (0, -1, 1),
]
WEIGHTS = [1.0 / 3.0] + [1.0 / 18.0] * 6 + [1.0 / 36.0] * 12
PAIRS = [(q, q + 1) for q in range(1, 19, 2)]
OPP = [0, 2, 1, 4, 3, 6, 5, 8, 7, 10, 9, 12, 11, 14, 13, 16, 15, 18, 17]
RELAX = 0.8
THIRDS = (0, 2, 1)
ORDER = [18, 5, 11, 14, 15, 17, 12, 13, 6, 16, 4, 8, 9, 1, 2, 0, 3, 7, 10]
SLOT = [ORDER.index(q) for q in range(19)]
LEFT_BIT = 19
RIGHT_BIT = 20


def tile_iota(axis, shape=(8, 128)):
    return lax.broadcasted_iota(jnp.int32, shape, axis)


def moments(f):
    d = {a: f[a] - f[b] for a, b in PAIRS}
    s = {a: f[a] + f[b] for a, b in PAIRS}
    density = (
        ((s[1] + s[3]) + (s[5] + s[7])) + ((s[9] + s[11]) + (s[13] + s[15])) + (s[17] + f[0])
    )
    mx = (d[1] + d[7]) + (d[9] + d[11]) + d[13]
    my = (d[3] + d[7]) + (d[15] - d[9]) + d[17]
    mz = (d[5] + d[11]) + (d[15] - d[13]) - d[17]
    inv = 1.0 / density
    return density, mx * inv, my * inv, mz * inv


def along(u, q):
    total = None
    for step, part in zip(DIRS[q], u):
        if step == 0:
            continue
        if total is None:
            total = part if step > 0 else -part
        else:
            total = total + part if step > 0 else total - part
    return total


def collide(f, gas):
    density, ux, uy, uz = moments(f)
    base = 1.0 - 1.5 * (ux * ux + uy * uy + uz * uz)
    triple = (3.0 * ux, 3.0 * uy, 3.0 * uz)
    kept = [None] * 19
    keep = 1.0 - RELAX
    scaled = {w: (RELAX * w) * density for w in (1.0 / 18.0, 1.0 / 36.0)}
    post = keep * f[0] + (RELAX / 3.0) * density * base
    kept[0] = jnp.where(gas, -f[0], post)
    for a, b in PAIRS:
        wd = scaled[WEIGHTS[a]]
        c = along(triple, a)
        even = wd * (base + 0.5 * (c * c))
        odd = wd * c
        kept[a] = jnp.where(gas, -f[b], keep * f[a] + (even + odd))
        kept[b] = jnp.where(gas, -f[a], keep * f[b] + (even - odd))
    zero = jnp.zeros_like(ux)
    velocity = [jnp.where(gas, zero, v) for v in (ux, uy, uz, base)]
    return kept, velocity


def shifted(load, step_x, step_y, left, right):
    lane = tile_iota(1)

    def flat(by):
        rows, lanes = by // 128, by % 128
        if lanes == 0:
            return load(-rows)
        picked = jnp.where(lane >= 128 - lanes, load(-rows - 1), load(-rows))
        return pltpu.roll(picked, lanes, 1)

    main = flat(step_x + ACROSS * step_y)
    if step_x == 0:
        return main
    by = step_x + ACROSS * step_y - ACROSS * step_x
    rows, lanes = by // 128, by % 128
    targets = (0, 64) if step_x == 1 else (63, 127)
    if all(t < lanes for t in targets):
        wrapped = pltpu.roll(load(-rows - 1), lanes, 1)
    elif all(t >= lanes for t in targets):
        wrapped = pltpu.roll(load(-rows), lanes, 1)
    else:
        wrapped = flat(by)
    return jnp.where(left if step_x == 1 else right, wrapped, main)


def window(ref, lead, z, rb):
    def load(n):
        return ref[(*lead, z, pl.ds(rb * 8 + (PAD + n), 8), slice(None))]

    return load


def passed(post_ref, mask_ref, vel_ref, z, rb):
    mask = mask_ref[z, pl.ds(rb * 8, 8), :]
    left = (mask & (1 << LEFT_BIT)) != 0
    right = (mask & (1 << RIGHT_BIT)) != 0
    ux, uy, uz, base = [vel_ref[i, z, pl.ds(rb * 8, 8), :] for i in range(4)]
    centre = [post_ref[SLOT[q], z + 1, pl.ds(rb * 8 + PAD, 8), :] for q in range(19)]
    new = [None] * 19
    new[0] = jnp.where((mask & 1) != 0, -centre[0], centre[0])
    triple = (3.0 * ux, 3.0 * uy, 3.0 * uz)
    for a, b in PAIRS:
        c = along(triple, a)
        both = (2.0 * WEIGHTS[a]) * (base + 0.5 * (c * c))
        for q, back in ((a, b), (b, a)):
            step_x, step_y, step_z = DIRS[q]
            source = shifted(
                window(post_ref, (SLOT[q],), z + 1 - step_z, rb), step_x, step_y, left, right
            )
            new[q] = jnp.where((mask & (1 << q)) != 0, both - centre[back], source)
    return new, (mask & 1) != 0


def two_terms(x):
    high = x.astype(jnp.bfloat16)
    low = (x - high.astype(jnp.float32)).astype(jnp.bfloat16)
    return jnp.concatenate([high, low], axis=1)


def pick(one_hot, values):
    both = jnp.dot(one_hot, two_terms(values), preferred_element_type=jnp.float32)
    return both[:, :128] + both[:, 128:]


def inner_tile(j):
    return 1 + lax.div(j, 7), 1 + lax.rem(j, 7)


def side_tile(j):
    return 1 + lax.div(j, 2), lax.rem(j, 2) * 8


def face_tile(first_rb, count):
    return lambda j: (lax.div(j, count) * 3, first_rb + lax.rem(j, count))


def any_tile(j):
    return lax.div(j, 9), lax.rem(j, 9)


def over(tile, count, body, unroll=None):
    def step(j, carry):
        body(*tile(j))
        return carry

    lax.fori_loop(0, count, step, 0, unroll=unroll or count)


def kernel(
    pop_hbm,
    kind_hbm,
    temp_hbm,
    line_hbm,
    want_hbm,
    place_hbm,
    hits_hbm,
    beam_hbm,
    field,
    thermal,
    cells,
    inputs,
    kind,
    temp,
    line,
    want,
    place,
    hits,
    beam,
    gas_pad,
    post1,
    post2,
    mask,
    vel,
    ask_send,
    ask_mid,
    ask_recv,
    row_send,
    row_recv,
    heat_send,
    heat_recv,
    slot_hot,
    ray_hot,
    cell_hot,
    back_hot,
    ray_rows,
    live,
    load_sem,
    small_sem,
    gas_s,
    gas_r,
    halo_s,
    halo_r,
    all_s,
    all_r,
    th_s,
    th_r,
):
    gz = lax.axis_index("gz")
    gy = lax.axis_index("gy")
    up, down = lax.rem(gz + 1, N_GZ), lax.rem(gz + N_GZ - 1, N_GZ)
    north, south = lax.rem(gy + 1, N_GY), lax.rem(gy + N_GY - 1, N_GY)

    barrier = pltpu.get_barrier_semaphore()

    def greet(i, carry):
        pl.semaphore_signal(
            barrier, 1, device_id=(lax.rem(gz + i, N_GZ), gy), device_id_type=MESH
        )
        return carry

    lax.fori_loop(1, N_GZ, greet, 0, unroll=N_GZ - 1)
    for i in range(1, N_GY):
        pl.semaphore_signal(barrier, 1, device_id=(gz, lax.rem(gy + i, N_GY)), device_id_type=MESH)
    for peer in ((up, north), (up, south), (down, north), (down, south)):
        pl.semaphore_signal(barrier, 1, device_id=peer, device_id_type=MESH)

    kind_copy = pltpu.make_async_copy(kind_hbm, kind, small_sem.at[6])
    kind_copy.start()
    want_copy = pltpu.make_async_copy(want_hbm, want, small_sem.at[5])
    want_copy.start()

    def part(rb):
        rows = pl.ds(rb * 32, 32)
        return pltpu.make_async_copy(pop_hbm.at[:, rows], inputs.at[:, rows], load_sem.at[rb])

    for third in THIRDS:
        for rb in range(3 * third, 3 * third + 3):
            part(rb).start()

    small = []
    for i, (src, dst) in enumerate(
        (
            (line_hbm, line),
            (place_hbm, place),
            (hits_hbm, hits),
            (beam_hbm, beam),
            (temp_hbm, temp),
        )
    ):
        copy = pltpu.make_async_copy(src, dst, small_sem.at[i])
        copy.start()
        small.append(copy)

    kind_copy.wait()

    def flags(z, rb):
        gas = kind[pl.ds(rb * 32 + z, 8, stride=DEPTH), :] == 0
        gas_pad[z + 1, pl.ds(rb * 8 + PAD, 8), :] = gas.astype(jnp.int32)

    over(any_tile, 36, flags, 12)

    want_copy.wait()
    row, lane = tile_iota(0, (DEVICES, DEVICES)), tile_iota(1, (DEVICES, DEVICES))
    holder = lane == (row & (N_GZ - 1)) * N_GY + (row >> 5)
    rows_of = jnp.zeros((DEVICES, DEVICES), jnp.float32)
    for s in range(CAP):
        asked = want[s : s + 1, :].astype(jnp.float32)
        column = jnp.sum(jnp.where(holder, asked, 0.0), axis=1, keepdims=True)
        rows_of = jnp.where(lane == s, column, rows_of)
    ask_send[...] = rows_of.reshape(N_GY, N_GZ, DEVICES)
    ask_mid[gy] = ask_send[gy]

    low_src, low_dst = slice(PAD, PAD + 2), slice(PAD + ROWS, PAD + ROWS + 2)
    high_src, high_dst = slice(PAD + ROWS - 2, PAD + ROWS), slice(PAD - 2, PAD)
    body = slice(PAD, PAD + ROWS)
    planes = slice(1, 1 + DEPTH)

    def send(ref, src, dst, s, r, peer):
        copy = pltpu.make_async_remote_copy(
            src_ref=ref.at[src],
            dst_ref=ref.at[dst],
            send_sem=s,
            recv_sem=r,
            device_id=peer,
            device_id_type=MESH,
        )
        copy.start()
        return copy

    def face_moves(first_rb, count):
        rows = slice(PAD + 8 * first_rb, PAD + 8 * (first_rb + count))
        return (
            ((slice(0, 5), 4, rows), (slice(0, 5), 0, rows), (up, gy)),
            ((slice(5, 10), 1, rows), (slice(5, 10), 5, rows), (down, gy)),
        )

    side_moves = (
        ((slice(4, 6), planes, high_src), (slice(4, 6), planes, high_dst), (gz, north)),
        ((slice(16, 19), planes, high_src), (slice(16, 19), planes, high_dst), (gz, north)),
        ((slice(9, 13), planes, low_src), (slice(9, 13), planes, low_dst), (gz, south)),
        ((slice(0, 1), planes, low_src), (slice(0, 1), planes, low_dst), (gz, south)),
    )
    corner_moves = (
        ((4, 4, high_src), (4, 0, high_dst), (up, north)),
        ((9, 1, low_src), (9, 5, low_dst), (down, south)),
        ((5, 1, high_src), (5, 5, high_dst), (down, north)),
        ((0, 4, low_src), (0, 0, low_dst), (up, south)),
    )

    def send_all(ref, moves, s, r, first_sem):
        return [
            send(ref, src, dst, s.at[first_sem + i], r.at[first_sem + i], peer)
            for i, (src, dst, peer) in enumerate(moves)
        ]

    gas_moves = (
        ((4, body), (0, body), (up, gy)),
        ((1, body), (5, body), (down, gy)),
        ((planes, high_src), (planes, high_dst), (gz, north)),
        ((planes, low_src), (planes, low_dst), (gz, south)),
        ((4, high_src), (0, high_dst), (up, north)),
        ((4, low_src), (0, low_dst), (up, south)),
        ((1, high_src), (5, high_dst), (down, north)),
        ((1, low_src), (5, low_dst), (down, south)),
    )

    def first(z, rb):
        rows = pl.ds(rb * 32 + z, 8, stride=DEPTH)
        kept, velocity = collide([inputs[q, rows, :] for q in range(19)], kind[rows, :] == 0)
        for q in range(19):
            post1[SLOT[q], z + 1, pl.ds(rb * 8 + PAD, 8), :] = kept[q]
        for i in range(4):
            vel[i, z, pl.ds(rb * 8, 8), :] = velocity[i]

    def ask_row():
        for i in range(1, N_GY):
            peer = lax.rem(gy + i, N_GY)
            pltpu.make_async_remote_copy(
                src_ref=ask_send.at[peer],
                dst_ref=ask_mid.at[gy],
                send_sem=all_s.at[0],
                recv_sem=all_r.at[0],
                device_id=(gz, peer),
                device_id_type=MESH,
            ).start()

    pl.semaphore_wait(barrier, N_GZ - 1 + N_GY - 1 + 4)
    gas_copies = send_all(gas_pad, gas_moves, gas_s, gas_r, 0)
    ask_row()
    faces1 = []
    for third in THIRDS:
        for rb in range(3 * third, 3 * third + 3):
            part(rb).wait()
        over(lambda j: (lax.div(j, 3), 3 * third + lax.rem(j, 3)), 12, first)
        faces1.append(send_all(post1, face_moves(3 * third, 3), halo_s, halo_r, 2 * third))
        if third == THIRDS[1]:
            corners1 = send_all(post1, corner_moves, halo_s, halo_r, 10)
            sides1 = send_all(post1, side_moves, halo_s, halo_r, 6)
    for copy in small:
        copy.wait()

    def ask_columns():
        pltpu.make_async_copy(
            ask_send.at[: N_GY - 1], ask_mid.at[: N_GY - 1], all_r.at[0]
        ).wait()
        ask_recv[:, pl.ds(gz, 1), :] = ask_mid[:, pl.ds(gz, 1), :]

        def ask(i, carry):
            peer = lax.rem(gz + i, N_GZ)
            pltpu.make_async_remote_copy(
                src_ref=ask_mid.at[:, pl.ds(peer, 1)],
                dst_ref=ask_recv.at[:, pl.ds(gz, 1)],
                send_sem=all_s.at[3],
                recv_sem=all_r.at[3],
                device_id=(peer, gy),
                device_id_type=MESH,
            ).start()
            return carry

        lax.fori_loop(1, N_GZ, ask, 0, unroll=N_GZ - 1)

    def masks(z, rb):
        place_x = lax.rem(
            (rb * 8 + tile_iota(0)) * 128 + tile_iota(1), jnp.full((8, 128), ACROSS, jnp.int32)
        )
        left, right = place_x == 0, place_x == ACROSS - 1
        own = gas_pad[z + 1, pl.ds(rb * 8 + PAD, 8), :]
        bits = own
        for q in range(1, 19):
            step_x, step_y, step_z = DIRS[q]
            source = shifted(window(gas_pad, (), z + 1 - step_z, rb), step_x, step_y, left, right)
            bits = bits | (jnp.maximum(source, own) << q)
        bits = bits | (left.astype(jnp.int32) << LEFT_BIT) | (right.astype(jnp.int32) << RIGHT_BIT)
        mask[z, pl.ds(rb * 8, 8), :] = bits

    def second(z, rb):
        new, gas = passed(post1, mask, vel, z, rb)
        kept, velocity = collide(new, gas)
        for q in range(19):
            post2[SLOT[q], z + 1, pl.ds(rb * 8 + PAD, 8), :] = kept[q]
        for i in range(4):
            vel[i, z, pl.ds(rb * 8, 8), :] = velocity[i]

    over(inner_tile, 14, masks, 7)
    over(inner_tile, 14, second, 7)
    ask_columns()
    for copy in gas_copies:
        copy.wait()
    over(side_tile, 4, masks)
    over(face_tile(0, 9), 18, masks, 9)
    for copy in sides1:
        copy.wait()
    over(side_tile, 4, second)
    faces2 = []

    def second_faces(first_rb, count):
        over(face_tile(first_rb, count), 2 * count, second)

    def send_faces(first_rb, count):
        faces2.append(
            send_all(post2, face_moves(first_rb, count), halo_s, halo_r, 14 + 2 * len(faces2))
        )

    for copy in faces1[0]:
        copy.wait()
    second_faces(1, 1)
    for copy in faces1[1]:
        copy.wait()
    second_faces(7, 1)
    for copy in corners1:
        copy.wait()
    second_faces(0, 1)
    send_faces(0, 2)
    second_faces(8, 1)
    send_faces(7, 2)
    corners2 = send_all(post2, corner_moves, halo_s, halo_r, 26)
    sides2 = send_all(post2, side_moves, halo_s, halo_r, 22)
    for copy in faces1[2]:
        copy.wait()
    second_faces(2, 3)
    send_faces(2, 3)
    second_faces(5, 2)
    send_faces(5, 2)

    big0, big1 = tile_iota(0, (SLOTS, SLOTS)), tile_iota(1, (SLOTS, SLOTS))
    diagonal = big0 == big1
    spot = place[...]
    spot = (spot & 3) * DEVICES + ((spot >> 2) & 3) * N_GZ + (spot >> 4)
    slot_hot[...] = (big0 == spot).astype(jnp.float32).astype(jnp.bfloat16)
    spot_col = jnp.sum(
        jnp.where(diagonal, spot.astype(jnp.float32), 0.0), axis=1, keepdims=True
    )
    ray_hot[...] = (big1.astype(jnp.float32) == spot_col).astype(jnp.float32).astype(jnp.bfloat16)
    eye_rays = tile_iota(0, (RAYS, RAYS)) == tile_iota(1, (RAYS, RAYS))
    live[...] = jnp.broadcast_to(
        jnp.sum(jnp.where(eye_rays, hits[...].astype(jnp.float32), 0.0), axis=1, keepdims=True),
        (RAYS, 128),
    )
    others = ask_recv.at[:, : N_GZ - 1]
    pltpu.make_async_copy(others, others, all_r.at[3]).wait()
    asked_rows = ask_recv[...].reshape(DEVICES, DEVICES)
    block = tile_iota(1, (DEVICES, NB_DEV)).astype(jnp.float32)
    lines = line[...].astype(jnp.float32)
    wanted_row = []
    for s in range(CAP):
        chosen = asked_rows[:, s : s + 1] == block
        wanted_row.append(jnp.sum(jnp.where(chosen, lines, 0.0), axis=1, keepdims=True))
    row_col = jnp.concatenate(wanted_row, axis=0)
    cell_hot[...] = (
        (tile_iota(1, (SLOTS, 384)).astype(jnp.float32) == row_col)
        .astype(jnp.float32)
        .astype(jnp.bfloat16)
    )
    row_row = jnp.sum(jnp.where(diagonal, row_col, 0.0), axis=0, keepdims=True)
    back_hot[...] = (
        (tile_iota(0, (CELL_ROWS, SLOTS)).astype(jnp.float32) == row_row)
        .astype(jnp.float32)
        .astype(jnp.bfloat16)
    )
    cells[CELL_ROWS:, :] = jnp.zeros((384 - CELL_ROWS, 128), jnp.float32)

    def last(z, rb):
        new, gas = passed(post2, mask, vel, z, rb)
        rows = pl.ds(rb * 32 + z, 8, stride=DEPTH)
        for q in range(19):
            field[q, rows, :] = new[q]
        density, ux, uy, uz = moments(new)
        for i, v in enumerate((ux, uy, uz)):
            vel[i, z, pl.ds(rb * 8, 8), :] = v
        cosine = 0.2 + 0.7 / (1.0 + jnp.exp(-8.0 * (density - 1.0)))
        index = 1.0 + temp[rows, :]
        upper = (index - cosine) * (index - cosine) + 1.0
        lower = (index + cosine) * (index + cosine) + 1.0
        cells[pl.ds(pl.multiple_of(z * ROWS + rb * 8, 8), 8), :] = jnp.where(
            gas, 1.0, upper / lower
        )

    over(inner_tile, 14, last, 7)
    for copy in sides2:
        copy.wait()
    over(side_tile, 4, last)
    for copy in faces2[0] + faces2[1] + corners2:
        copy.wait()
    over(face_tile(0, 1), 2, last)
    over(face_tile(8, 1), 2, last)
    for copy in faces2[2]:
        copy.wait()
    over(face_tile(1, 3), 6, last)
    for copy in faces2[3]:
        copy.wait()
    over(face_tile(4, 4), 8, last)

    place_x, place_y = lax.div(gz, 8), lax.rem(lax.div(gz, 2), 4)
    core = lax.rem(gz, 2)
    x_on = [lax.rem(place_x + i, 4) * 8 for i in range(4)]
    y_on = [lax.rem(place_y + i, 4) * 2 for i in range(4)]
    cores = (core, 1 - core)
    me = gy * N_GZ + gz

    z_on = [lax.rem(gy + i, N_GY) for i in range(4)]

    def chips(partner):
        return sum(min(step, 4 - step) for step in partner[:3])

    partners = [
        ((7 * i) % 4, (i // 4 + i) % 4, (i // 16 + i // 4) % 4, other)
        for i in range(64)
        for other in (1, 0)
    ]
    partners = sorted(set(partners) - {(0, 0, 0, 0)}, key=lambda p: (-chips(p), partners.index(p)))
    assert len(partners) == DEVICES - 1

    def to_all(src, dst, n):
        dst[:, pl.ds(me, 1), :] = src[:, pl.ds(me, 1), :]

        def to_one(column, z):
            pltpu.make_async_remote_copy(
                src_ref=src.at[:, pl.ds(z * N_GZ + column, 1)],
                dst_ref=dst.at[:, pl.ds(me, 1)],
                send_sem=all_s.at[n],
                recv_sem=all_r.at[n],
                device_id=(column, z),
                device_id_type=MESH,
            ).start()

        for x, y, z, other in partners:
            to_one(x_on[x] + y_on[y] + cores[other], z_on[z])
        pltpu.make_async_copy(
            src.at[:, pl.ds(0, DEVICES - 1)], dst.at[:, pl.ds(0, DEVICES - 1)], all_r.at[n]
        ).wait()

    row_send[...] = pick(cell_hot[...], cells[...]).reshape(CAP, DEVICES, 128)
    to_all(row_send, row_recv, 1)

    ray_rows[...] = pick(ray_hot[...], row_recv[...].reshape(SLOTS, 128))
    energy = beam[...]
    hit_count = live[...]
    for j in range(BOUNCES):
        at = pl.ds(j, RAYS, stride=BOUNCES)
        ratio = ray_rows[at, :]
        ray_rows[at, :] = jnp.where(hit_count > float(j), energy * (1.0 - ratio), 0.0)
        energy = energy * ratio
    heat_send[...] = pick(slot_hot[...], ray_rows[...]).reshape(CAP, DEVICES, 128)
    to_all(heat_send, heat_recv, 2)

    cells[pl.ds(0, CELL_ROWS), :] = pick(back_hot[...], heat_recv[...].reshape(SLOTS, 128))

    def sources(z, rb):
        at = pl.ds(pl.multiple_of(z * ROWS + rb * 8, 8), 8)
        source = temp[pl.ds(rb * 32 + z, 8, stride=DEPTH), :] + cells[at, :]
        eighth = 0.125 * source
        for i in range(3):
            moved = eighth * (4.0 * vel[i, z, pl.ds(rb * 8, 8), :])
            thermal[2 * i, z + 1, pl.ds(rb * 8 + PAD, 8), :] = eighth + moved
            thermal[2 * i + 1, z + 1, pl.ds(rb * 8 + PAD, 8), :] = eighth - moved
        cells[at, :] = 0.25 * source

    over(any_tile, 36, sources)
    th_moves = (
        ((4, 4, body), (4, 0, body), (up, gy)),
        ((5, 1, body), (5, 5, body), (down, gy)),
        ((2, planes, high_src), (2, planes, high_dst), (gz, north)),
        ((3, planes, low_src), (3, planes, low_dst), (gz, south)),
    )
    for copy in send_all(thermal, th_moves, th_s, th_r, 0):
        copy.wait()
    pltpu.make_async_copy(
        ask_send.at[: N_GY - 1], ask_mid.at[: N_GY - 1], all_s.at[0]
    ).wait()
    pltpu.make_async_copy(others, others, all_s.at[3]).wait()
    for n, ref in ((1, row_send), (2, heat_send)):
        done = ref.at[:, pl.ds(0, DEVICES - 1)]
        pltpu.make_async_copy(done, done, all_s.at[n]).wait()


def finish(field, thermal, cells, out_hbm, temp_out_hbm, temp_out, out_sem, temp_sem):
    copies = []
    for i, (lo, hi) in enumerate(((0, 5), (5, 10), (10, 15), (15, 19))):
        copy = pltpu.make_async_copy(field.at[lo:hi], out_hbm.at[lo:hi], out_sem.at[i])
        copy.start()
        copies.append(copy)

    def gather(z, rb):
        place_x = lax.rem(
            (rb * 8 + tile_iota(0)) * 128 + tile_iota(1), jnp.full((8, 128), ACROSS, jnp.int32)
        )
        left, right = place_x == 0, place_x == ACROSS - 1
        total = cells[pl.ds(pl.multiple_of(z * ROWS + rb * 8, 8), 8), :]
        for i in range(6):
            step_x, step_y, step_z = DIRS[i + 1]
            total = total + shifted(
                window(thermal, (i,), z + 1 - step_z, rb), step_x, step_y, left, right
            )
        temp_out[pl.ds(rb * 32 + z, 8, stride=DEPTH), :] = total

    over(lambda j: (lax.rem(j, 4), lax.div(j, 4)), 36, gather, 12)
    copy = pltpu.make_async_copy(temp_out, temp_out_hbm, temp_sem)
    copy.start()
    copy.wait()
    for copy in copies:
        copy.wait()


def fold(x):
    lead = x.shape[:-2]
    n = len(lead)
    x = x.reshape(lead + (DEPTH, ROWS, 128)).transpose(tuple(range(n)) + (n + 1, n, n + 2))
    return x.reshape(lead + (CELL_ROWS, 128))


def unfold(x):
    lead = x.shape[:-2]
    n = len(lead)
    x = x.reshape(lead + (ROWS, DEPTH, 128)).transpose(tuple(range(n)) + (n + 1, n, n + 2))
    return x.reshape(lead + (DEPTH, ROWS * 128))


def per_device(populations, kinds, temperature, lines, wanted, places, hits, beam):
    f32, i32, bf16 = jnp.float32, jnp.int32, jnp.bfloat16
    dma = pltpu.SemaphoreType.DMA
    vmem = pl.BlockSpec(memory_space=pltpu.VMEM)
    whole = pl.BlockSpec(memory_space=pl.ANY)
    operands = (
        fold(populations),
        fold(kinds),
        fold(temperature),
        lines,
        wanted[0].T,
        places,
        hits,
        beam[0],
    )
    field, thermal, cells = pl.pallas_call(
        kernel,
        out_shape=(
            pltpu.VMEM((19, CELL_ROWS, 128), f32),
            pltpu.VMEM((6, DEPTH + 2, PLANE, 128), f32),
            pltpu.VMEM((384, 128), f32),
        ),
        in_specs=[whole] * 8,
        out_specs=[vmem] * 3,
        scratch_shapes=[
            pltpu.VMEM((19, CELL_ROWS, 128), f32),
            pltpu.VMEM((CELL_ROWS, 128), i32),
            pltpu.VMEM((CELL_ROWS, 128), f32),
            pltpu.VMEM((1, NB_DEV), i32),
            pltpu.VMEM((CAP, DEVICES), i32),
            pltpu.VMEM((1, SLOTS), i32),
            pltpu.VMEM((1, RAYS), i32),
            pltpu.VMEM((RAYS, 128), f32),
            pltpu.VMEM((DEPTH + 2, PLANE, 128), i32),
            pltpu.VMEM((19, DEPTH + 2, PLANE, 128), f32),
            pltpu.VMEM((19, DEPTH + 2, PLANE, 128), f32),
            pltpu.VMEM((DEPTH, ROWS, 128), i32),
            pltpu.VMEM((4, DEPTH, ROWS, 128), f32),
            pltpu.VMEM((N_GY, N_GZ, 128), f32),
            pltpu.VMEM((N_GY, N_GZ, 128), f32),
            pltpu.VMEM((N_GY, N_GZ, 128), f32),
            pltpu.VMEM((CAP, DEVICES, 128), f32),
            pltpu.VMEM((CAP, DEVICES, 128), f32),
            pltpu.VMEM((CAP, DEVICES, 128), f32),
            pltpu.VMEM((CAP, DEVICES, 128), f32),
            pltpu.VMEM((SLOTS, SLOTS), bf16),
            pltpu.VMEM((SLOTS, SLOTS), bf16),
            pltpu.VMEM((SLOTS, 384), bf16),
            pltpu.VMEM((CELL_ROWS, SLOTS), bf16),
            pltpu.VMEM((SLOTS, 128), f32),
            pltpu.VMEM((RAYS, 128), f32),
            dma((9,)),
            dma((7,)),
            dma((8,)),
            dma((8,)),
            dma((30,)),
            dma((30,)),
            dma((4,)),
            dma((4,)),
            dma((4,)),
            dma((4,)),
        ],
        compiler_params=pltpu.CompilerParams(
            collective_id=0, has_side_effects=True, vmem_limit_bytes=40 * 2**20
        ),
        cost_estimate=pl.CostEstimate(
            flops=100_000_000, bytes_accessed=7_000_000, transcendentals=40_000
        ),
    )(*[pltpu.with_memory_space_constraint(x, pltpu.HBM) for x in operands])
    lattice, heated = pl.pallas_call(
        finish,
        out_shape=(
            jax.ShapeDtypeStruct((19, CELL_ROWS, 128), f32),
            jax.ShapeDtypeStruct((CELL_ROWS, 128), f32),
        ),
        in_specs=[vmem] * 3,
        out_specs=[whole] * 2,
        scratch_shapes=[pltpu.VMEM((CELL_ROWS, 128), f32), dma((4,)), dma],
        compiler_params=pltpu.CompilerParams(vmem_limit_bytes=40 * 2**20),
        cost_estimate=pl.CostEstimate(
            flops=1_000_000, bytes_accessed=7_000_000, transcendentals=0
        ),
    )(*[pltpu.with_memory_space_constraint(x, pltpu.VMEM) for x in (field, thermal, cells)])
    return unfold(lattice), unfold(heated)


def solution(mesh):
    placed = (
        P(None, "gz", "gy"),
        P("gz", "gy"),
        P("gz", "gy"),
        P(("gz", "gy"), None),
        P(("gz", "gy"), None, None),
        P(("gz", "gy"), None),
        P(("gz", "gy"), None),
        P(("gz", "gy"), None, None),
    )
    return jax.shard_map(
        per_device,
        mesh=mesh,
        in_specs=placed,
        out_specs=(P(None, "gz", "gy"), P("gz", "gy")),
        check_vma=False,
    )
```

```python
import jax
import jax.numpy as jnp
from jax import lax
from jax.experimental import pallas as pl
from jax.experimental.pallas import tpu as pltpu
from jax.sharding import PartitionSpec as P

MESH = pl.DeviceIdType.MESH
N_GZ = 32
N_GY = 4
DEVICES = 128
CAP = 4
SLOTS = 512
NB_DEV = 64
RAYS = 64
BOUNCES = 8
ACROSS = 192
DEPTH = 4
ROWS = 72
CELL_ROWS = 288
PAD = 8
PLANE = ROWS + 2 * PAD

DIRS = [
    (0, 0, 0),
    (1, 0, 0),
    (-1, 0, 0),
    (0, 1, 0),
    (0, -1, 0),
    (0, 0, 1),
    (0, 0, -1),
    (1, 1, 0),
    (-1, -1, 0),
    (1, -1, 0),
    (-1, 1, 0),
    (1, 0, 1),
    (-1, 0, -1),
    (1, 0, -1),
    (-1, 0, 1),
    (0, 1, 1),
    (0, -1, -1),
    (0, 1, -1),
    (0, -1, 1),
]
WEIGHTS = [1.0 / 3.0] + [1.0 / 18.0] * 6 + [1.0 / 36.0] * 12
PAIRS = [(q, q + 1) for q in range(1, 19, 2)]
OPP = [0, 2, 1, 4, 3, 6, 5, 8, 7, 10, 9, 12, 11, 14, 13, 16, 15, 18, 17]
RELAX = 0.8
THIRDS = (0, 2, 1)
ORDER = [18, 5, 11, 14, 15, 17, 12, 13, 6, 16, 4, 8, 9, 1, 2, 0, 3, 7, 10]
SLOT = [ORDER.index(q) for q in range(19)]
LEFT_BIT = 19
RIGHT_BIT = 20


def tile_iota(axis, shape=(8, 128)):
    return lax.broadcasted_iota(jnp.int32, shape, axis)


def moments(f):
    d = {a: f[a] - f[b] for a, b in PAIRS}
    s = {a: f[a] + f[b] for a, b in PAIRS}
    density = (
        ((s[1] + s[3]) + (s[5] + s[7])) + ((s[9] + s[11]) + (s[13] + s[15])) + (s[17] + f[0])
    )
    mx = (d[1] + d[7]) + (d[9] + d[11]) + d[13]
    my = (d[3] + d[7]) + (d[15] - d[9]) + d[17]
    mz = (d[5] + d[11]) + (d[15] - d[13]) - d[17]
    inv = 1.0 / density
    return density, mx * inv, my * inv, mz * inv


def along(u, q):
    total = None
    for step, part in zip(DIRS[q], u):
        if step == 0:
            continue
        if total is None:
            total = part if step > 0 else -part
        else:
            total = total + part if step > 0 else total - part
    return total


def collide(f, gas):
    density, ux, uy, uz = moments(f)
    base = 1.0 - 1.5 * (ux * ux + uy * uy + uz * uz)
    triple = (3.0 * ux, 3.0 * uy, 3.0 * uz)
    kept = [None] * 19
    keep = 1.0 - RELAX
    scaled = {w: (RELAX * w) * density for w in (1.0 / 18.0, 1.0 / 36.0)}
    post = keep * f[0] + (RELAX / 3.0) * density * base
    kept[0] = jnp.where(gas, -f[0], post)
    for a, b in PAIRS:
        wd = scaled[WEIGHTS[a]]
        c = along(triple, a)
        even = wd * (base + 0.5 * (c * c))
        odd = wd * c
        kept[a] = jnp.where(gas, -f[b], keep * f[a] + (even + odd))
        kept[b] = jnp.where(gas, -f[a], keep * f[b] + (even - odd))
    zero = jnp.zeros_like(ux)
    velocity = [jnp.where(gas, zero, v) for v in (ux, uy, uz, base)]
    return kept, velocity


def shifted(load, step_x, step_y, left, right):
    lane = tile_iota(1)

    def flat(by):
        rows, lanes = by // 128, by % 128
        if lanes == 0:
            return load(-rows)
        picked = jnp.where(lane >= 128 - lanes, load(-rows - 1), load(-rows))
        return pltpu.roll(picked, lanes, 1)

    main = flat(step_x + ACROSS * step_y)
    if step_x == 0:
        return main
    by = step_x + ACROSS * step_y - ACROSS * step_x
    rows, lanes = by // 128, by % 128
    targets = (0, 64) if step_x == 1 else (63, 127)
    if all(t < lanes for t in targets):
        wrapped = pltpu.roll(load(-rows - 1), lanes, 1)
    elif all(t >= lanes for t in targets):
        wrapped = pltpu.roll(load(-rows), lanes, 1)
    else:
        wrapped = flat(by)
    return jnp.where(left if step_x == 1 else right, wrapped, main)


def window(ref, lead, z, rb):
    def load(n):
        return ref[(*lead, z, pl.ds(rb * 8 + (PAD + n), 8), slice(None))]

    return load


def passed(post_ref, mask_ref, vel_ref, z, rb):
    mask = mask_ref[z, pl.ds(rb * 8, 8), :]
    left = (mask & (1 << LEFT_BIT)) != 0
    right = (mask & (1 << RIGHT_BIT)) != 0
    ux, uy, uz, base = [vel_ref[i, z, pl.ds(rb * 8, 8), :] for i in range(4)]
    centre = [post_ref[SLOT[q], z + 1, pl.ds(rb * 8 + PAD, 8), :] for q in range(19)]
    new = [None] * 19
    new[0] = jnp.where((mask & 1) != 0, -centre[0], centre[0])
    triple = (3.0 * ux, 3.0 * uy, 3.0 * uz)
    for a, b in PAIRS:
        c = along(triple, a)
        both = (2.0 * WEIGHTS[a]) * (base + 0.5 * (c * c))
        for q, back in ((a, b), (b, a)):
            step_x, step_y, step_z = DIRS[q]
            source = shifted(
                window(post_ref, (SLOT[q],), z + 1 - step_z, rb), step_x, step_y, left, right
            )
            new[q] = jnp.where((mask & (1 << q)) != 0, both - centre[back], source)
    return new, (mask & 1) != 0


def two_terms(x):
    high = x.astype(jnp.bfloat16)
    low = (x - high.astype(jnp.float32)).astype(jnp.bfloat16)
    return jnp.concatenate([high, low], axis=1)


def pick(one_hot, values):
    both = jnp.dot(one_hot, two_terms(values), preferred_element_type=jnp.float32)
    return both[:, :128] + both[:, 128:]


def inner_tile(j):
    return 1 + lax.div(j, 7), 1 + lax.rem(j, 7)


def side_tile(j):
    return 1 + lax.div(j, 2), lax.rem(j, 2) * 8


def face_tile(first_rb, count):
    return lambda j: (lax.div(j, count) * 3, first_rb + lax.rem(j, count))


def any_tile(j):
    return lax.div(j, 9), lax.rem(j, 9)


def over(tile, count, body, unroll=None):
    def step(j, carry):
        body(*tile(j))
        return carry

    lax.fori_loop(0, count, step, 0, unroll=unroll or count)


def kernel(
    pop_hbm,
    kind_hbm,
    temp_hbm,
    line_hbm,
    want_hbm,
    place_hbm,
    hits_hbm,
    beam_hbm,
    field,
    thermal,
    cells,
    inputs,
    kind,
    temp,
    line,
    want,
    place,
    hits,
    beam,
    gas_pad,
    post1,
    post2,
    mask,
    vel,
    ask_send,
    ask_mid,
    ask_recv,
    row_send,
    row_recv,
    heat_send,
    heat_recv,
    slot_hot,
    ray_hot,
    cell_hot,
    back_hot,
    ray_rows,
    live,
    load_sem,
    small_sem,
    gas_s,
    gas_r,
    halo_s,
    halo_r,
    all_s,
    all_r,
    th_s,
    th_r,
):
    gz = lax.axis_index("gz")
    gy = lax.axis_index("gy")
    up, down = lax.rem(gz + 1, N_GZ), lax.rem(gz + N_GZ - 1, N_GZ)
    north, south = lax.rem(gy + 1, N_GY), lax.rem(gy + N_GY - 1, N_GY)

    barrier = pltpu.get_barrier_semaphore()

    def greet(i, carry):
        pl.semaphore_signal(
            barrier, 1, device_id=(lax.rem(gz + i, N_GZ), gy), device_id_type=MESH
        )
        return carry

    lax.fori_loop(1, N_GZ, greet, 0, unroll=N_GZ - 1)
    for i in range(1, N_GY):
        pl.semaphore_signal(barrier, 1, device_id=(gz, lax.rem(gy + i, N_GY)), device_id_type=MESH)
    for peer in ((up, north), (up, south), (down, north), (down, south)):
        pl.semaphore_signal(barrier, 1, device_id=peer, device_id_type=MESH)

    kind_copy = pltpu.make_async_copy(kind_hbm, kind, small_sem.at[6])
    kind_copy.start()
    want_copy = pltpu.make_async_copy(want_hbm, want, small_sem.at[5])
    want_copy.start()

    def part(rb):
        rows = pl.ds(rb * 32, 32)
        return pltpu.make_async_copy(pop_hbm.at[:, rows], inputs.at[:, rows], load_sem.at[rb])

    for third in THIRDS:
        for rb in range(3 * third, 3 * third + 3):
            part(rb).start()

    small = []
    for i, (src, dst) in enumerate(
        (
            (line_hbm, line),
            (place_hbm, place),
            (hits_hbm, hits),
            (beam_hbm, beam),
            (temp_hbm, temp),
        )
    ):
        copy = pltpu.make_async_copy(src, dst, small_sem.at[i])
        copy.start()
        small.append(copy)

    kind_copy.wait()

    def flags(z, rb):
        gas = kind[pl.ds(rb * 32 + z, 8, stride=DEPTH), :] == 0
        gas_pad[z + 1, pl.ds(rb * 8 + PAD, 8), :] = gas.astype(jnp.int32)

    over(any_tile, 36, flags, 12)

    want_copy.wait()
    row, lane = tile_iota(0, (DEVICES, DEVICES)), tile_iota(1, (DEVICES, DEVICES))
    holder = lane == (row & (N_GZ - 1)) * N_GY + (row >> 5)
    rows_of = jnp.zeros((DEVICES, DEVICES), jnp.float32)
    for s in range(CAP):
        asked = want[s : s + 1, :].astype(jnp.float32)
        column = jnp.sum(jnp.where(holder, asked, 0.0), axis=1, keepdims=True)
        rows_of = jnp.where(lane == s, column, rows_of)
    ask_send[...] = rows_of.reshape(N_GY, N_GZ, DEVICES)
    ask_mid[gy] = ask_send[gy]

    low_src, low_dst = slice(PAD, PAD + 2), slice(PAD + ROWS, PAD + ROWS + 2)
    high_src, high_dst = slice(PAD + ROWS - 2, PAD + ROWS), slice(PAD - 2, PAD)
    body = slice(PAD, PAD + ROWS)
    planes = slice(1, 1 + DEPTH)

    def send(ref, src, dst, s, r, peer):
        copy = pltpu.make_async_remote_copy(
            src_ref=ref.at[src],
            dst_ref=ref.at[dst],
            send_sem=s,
            recv_sem=r,
            device_id=peer,
            device_id_type=MESH,
        )
        copy.start()
        return copy

    def face_moves(first_rb, count):
        rows = slice(PAD + 8 * first_rb, PAD + 8 * (first_rb + count))
        return (
            ((slice(0, 5), 4, rows), (slice(0, 5), 0, rows), (up, gy)),
            ((slice(5, 10), 1, rows), (slice(5, 10), 5, rows), (down, gy)),
        )

    side_moves = (
        ((slice(4, 6), planes, high_src), (slice(4, 6), planes, high_dst), (gz, north)),
        ((slice(16, 19), planes, high_src), (slice(16, 19), planes, high_dst), (gz, north)),
        ((slice(9, 13), planes, low_src), (slice(9, 13), planes, low_dst), (gz, south)),
        ((slice(0, 1), planes, low_src), (slice(0, 1), planes, low_dst), (gz, south)),
    )
    corner_moves = (
        ((4, 4, high_src), (4, 0, high_dst), (up, north)),
        ((9, 1, low_src), (9, 5, low_dst), (down, south)),
        ((5, 1, high_src), (5, 5, high_dst), (down, north)),
        ((0, 4, low_src), (0, 0, low_dst), (up, south)),
    )

    def send_all(ref, moves, s, r, first_sem):
        return [
            send(ref, src, dst, s.at[first_sem + i], r.at[first_sem + i], peer)
            for i, (src, dst, peer) in enumerate(moves)
        ]

    gas_moves = (
        ((4, body), (0, body), (up, gy)),
        ((1, body), (5, body), (down, gy)),
        ((planes, high_src), (planes, high_dst), (gz, north)),
        ((planes, low_src), (planes, low_dst), (gz, south)),
        ((4, high_src), (0, high_dst), (up, north)),
        ((4, low_src), (0, low_dst), (up, south)),
        ((1, high_src), (5, high_dst), (down, north)),
        ((1, low_src), (5, low_dst), (down, south)),
    )

    def first(z, rb):
        rows = pl.ds(rb * 32 + z, 8, stride=DEPTH)
        kept, velocity = collide([inputs[q, rows, :] for q in range(19)], kind[rows, :] == 0)
        for q in range(19):
            post1[SLOT[q], z + 1, pl.ds(rb * 8 + PAD, 8), :] = kept[q]
        for i in range(4):
            vel[i, z, pl.ds(rb * 8, 8), :] = velocity[i]

    def ask_row():
        for i in range(1, N_GY):
            peer = lax.rem(gy + i, N_GY)
            pltpu.make_async_remote_copy(
                src_ref=ask_send.at[peer],
                dst_ref=ask_mid.at[gy],
                send_sem=all_s.at[0],
                recv_sem=all_r.at[0],
                device_id=(gz, peer),
                device_id_type=MESH,
            ).start()

    pl.semaphore_wait(barrier, N_GZ - 1 + N_GY - 1 + 4)
    gas_copies = send_all(gas_pad, gas_moves, gas_s, gas_r, 0)
    ask_row()
    faces1 = []
    for third in THIRDS:
        for rb in range(3 * third, 3 * third + 3):
            part(rb).wait()
        over(lambda j: (lax.div(j, 3), 3 * third + lax.rem(j, 3)), 12, first)
        faces1.append(send_all(post1, face_moves(3 * third, 3), halo_s, halo_r, 2 * third))
        if third == THIRDS[1]:
            corners1 = send_all(post1, corner_moves, halo_s, halo_r, 10)
            sides1 = send_all(post1, side_moves, halo_s, halo_r, 6)
    for copy in small:
        copy.wait()

    def ask_columns():
        pltpu.make_async_copy(
            ask_send.at[: N_GY - 1], ask_mid.at[: N_GY - 1], all_r.at[0]
        ).wait()
        ask_recv[:, pl.ds(gz, 1), :] = ask_mid[:, pl.ds(gz, 1), :]

        def ask(i, carry):
            peer = lax.rem(gz + i, N_GZ)
            pltpu.make_async_remote_copy(
                src_ref=ask_mid.at[:, pl.ds(peer, 1)],
                dst_ref=ask_recv.at[:, pl.ds(gz, 1)],
                send_sem=all_s.at[3],
                recv_sem=all_r.at[3],
                device_id=(peer, gy),
                device_id_type=MESH,
            ).start()
            return carry

        lax.fori_loop(1, N_GZ, ask, 0, unroll=N_GZ - 1)

    def masks(z, rb):
        place_x = lax.rem(
            (rb * 8 + tile_iota(0)) * 128 + tile_iota(1), jnp.full((8, 128), ACROSS, jnp.int32)
        )
        left, right = place_x == 0, place_x == ACROSS - 1
        own = gas_pad[z + 1, pl.ds(rb * 8 + PAD, 8), :]
        bits = own
        for q in range(1, 19):
            step_x, step_y, step_z = DIRS[q]
            source = shifted(window(gas_pad, (), z + 1 - step_z, rb), step_x, step_y, left, right)
            bits = bits | (jnp.maximum(source, own) << q)
        bits = bits | (left.astype(jnp.int32) << LEFT_BIT) | (right.astype(jnp.int32) << RIGHT_BIT)
        mask[z, pl.ds(rb * 8, 8), :] = bits

    def second(z, rb):
        new, gas = passed(post1, mask, vel, z, rb)
        kept, velocity = collide(new, gas)
        for q in range(19):
            post2[SLOT[q], z + 1, pl.ds(rb * 8 + PAD, 8), :] = kept[q]
        for i in range(4):
            vel[i, z, pl.ds(rb * 8, 8), :] = velocity[i]

    over(inner_tile, 14, masks, 7)
    over(inner_tile, 14, second, 7)
    ask_columns()
    for copy in gas_copies:
        copy.wait()
    over(side_tile, 4, masks)
    over(face_tile(0, 9), 18, masks, 9)
    for copy in sides1:
        copy.wait()
    over(side_tile, 4, second)
    faces2 = []

    def second_faces(first_rb, count):
        over(face_tile(first_rb, count), 2 * count, second)

    def send_faces(first_rb, count):
        faces2.append(
            send_all(post2, face_moves(first_rb, count), halo_s, halo_r, 14 + 2 * len(faces2))
        )

    for copy in faces1[0]:
        copy.wait()
    second_faces(1, 1)
    for copy in faces1[1]:
        copy.wait()
    second_faces(7, 1)
    for copy in corners1:
        copy.wait()
    second_faces(0, 1)
    send_faces(0, 2)
    second_faces(8, 1)
    send_faces(7, 2)
    corners2 = send_all(post2, corner_moves, halo_s, halo_r, 26)
    sides2 = send_all(post2, side_moves, halo_s, halo_r, 22)
    for copy in faces1[2]:
        copy.wait()
    second_faces(2, 3)
    send_faces(2, 3)
    second_faces(5, 2)
    send_faces(5, 2)

    big0, big1 = tile_iota(0, (SLOTS, SLOTS)), tile_iota(1, (SLOTS, SLOTS))
    diagonal = big0 == big1
    spot = place[...]
    spot = (spot & 3) * DEVICES + ((spot >> 2) & 3) * N_GZ + (spot >> 4)
    slot_hot[...] = (big0 == spot).astype(jnp.float32).astype(jnp.bfloat16)
    spot_col = jnp.sum(
        jnp.where(diagonal, spot.astype(jnp.float32), 0.0), axis=1, keepdims=True
    )
    ray_hot[...] = (big1.astype(jnp.float32) == spot_col).astype(jnp.float32).astype(jnp.bfloat16)
    eye_rays = tile_iota(0, (RAYS, RAYS)) == tile_iota(1, (RAYS, RAYS))
    live[...] = jnp.broadcast_to(
        jnp.sum(jnp.where(eye_rays, hits[...].astype(jnp.float32), 0.0), axis=1, keepdims=True),
        (RAYS, 128),
    )
    others = ask_recv.at[:, : N_GZ - 1]
    pltpu.make_async_copy(others, others, all_r.at[3]).wait()
    asked_rows = ask_recv[...].reshape(DEVICES, DEVICES)
    block = tile_iota(1, (DEVICES, NB_DEV)).astype(jnp.float32)
    lines = line[...].astype(jnp.float32)
    wanted_row = []
    for s in range(CAP):
        chosen = asked_rows[:, s : s + 1] == block
        wanted_row.append(jnp.sum(jnp.where(chosen, lines, 0.0), axis=1, keepdims=True))
    row_col = jnp.concatenate(wanted_row, axis=0)
    cell_hot[...] = (
        (tile_iota(1, (SLOTS, 384)).astype(jnp.float32) == row_col)
        .astype(jnp.float32)
        .astype(jnp.bfloat16)
    )
    row_row = jnp.sum(jnp.where(diagonal, row_col, 0.0), axis=0, keepdims=True)
    back_hot[...] = (
        (tile_iota(0, (CELL_ROWS, SLOTS)).astype(jnp.float32) == row_row)
        .astype(jnp.float32)
        .astype(jnp.bfloat16)
    )
    cells[CELL_ROWS:, :] = jnp.zeros((384 - CELL_ROWS, 128), jnp.float32)

    def last(z, rb):
        new, gas = passed(post2, mask, vel, z, rb)
        rows = pl.ds(rb * 32 + z, 8, stride=DEPTH)
        for q in range(19):
            field[q, rows, :] = new[q]
        density, ux, uy, uz = moments(new)
        for i, v in enumerate((ux, uy, uz)):
            vel[i, z, pl.ds(rb * 8, 8), :] = v
        cosine = 0.2 + 0.7 / (1.0 + jnp.exp(-8.0 * (density - 1.0)))
        index = 1.0 + temp[rows, :]
        upper = (index - cosine) * (index - cosine) + 1.0
        lower = (index + cosine) * (index + cosine) + 1.0
        cells[pl.ds(pl.multiple_of(z * ROWS + rb * 8, 8), 8), :] = jnp.where(
            gas, 1.0, upper / lower
        )

    over(inner_tile, 14, last, 7)
    for copy in sides2:
        copy.wait()
    over(side_tile, 4, last)
    for copy in faces2[0] + faces2[1] + corners2:
        copy.wait()
    over(face_tile(0, 1), 2, last)
    over(face_tile(8, 1), 2, last)
    for copy in faces2[2]:
        copy.wait()
    over(face_tile(1, 3), 6, last)
    for copy in faces2[3]:
        copy.wait()
    over(face_tile(4, 4), 8, last)

    place_x, place_y = lax.div(gz, 8), lax.rem(lax.div(gz, 2), 4)
    core = lax.rem(gz, 2)
    x_on = [lax.rem(place_x + i, 4) * 8 for i in range(4)]
    y_on = [lax.rem(place_y + i, 4) * 2 for i in range(4)]
    cores = (core, 1 - core)
    me = gy * N_GZ + gz

    z_on = [lax.rem(gy + i, N_GY) for i in range(4)]

    def chips(partner):
        return sum(min(step, 4 - step) for step in partner[:3])

    partners = [
        ((7 * i) % 4, (i // 4 + i) % 4, (i // 16 + i // 4) % 4, other)
        for i in range(64)
        for other in (1, 0)
    ]
    partners = sorted(set(partners) - {(0, 0, 0, 0)}, key=lambda p: (-chips(p), partners.index(p)))
    assert len(partners) == DEVICES - 1

    def to_all(src, dst, n):

        def to_one(column, z):
            pltpu.make_async_remote_copy(
                src_ref=src.at[:, pl.ds(z * N_GZ + column, 1)],
                dst_ref=dst.at[:, pl.ds(me, 1)],
                send_sem=all_s.at[n],
                recv_sem=all_r.at[n],
                device_id=(column, z),
                device_id_type=MESH,
            ).start()

        for x, y, z, other in partners:
            to_one(x_on[x] + y_on[y] + cores[other], z_on[z])
        dst[:, pl.ds(me, 1), :] = src[:, pl.ds(me, 1), :]
        pltpu.make_async_copy(
            src.at[:, pl.ds(0, DEVICES - 1)], dst.at[:, pl.ds(0, DEVICES - 1)], all_r.at[n]
        ).wait()

    row_send[...] = pick(cell_hot[...], cells[...]).reshape(CAP, DEVICES, 128)
    to_all(row_send, row_recv, 1)

    ray_rows[...] = pick(ray_hot[...], row_recv[...].reshape(SLOTS, 128))
    energy = beam[...]
    hit_count = live[...]
    for j in range(BOUNCES):
        at = pl.ds(j, RAYS, stride=BOUNCES)
        ratio = ray_rows[at, :]
        ray_rows[at, :] = jnp.where(hit_count > float(j), energy * (1.0 - ratio), 0.0)
        energy = energy * ratio
    heat_send[...] = pick(slot_hot[...], ray_rows[...]).reshape(CAP, DEVICES, 128)
    to_all(heat_send, heat_recv, 2)

    cells[pl.ds(0, CELL_ROWS), :] = pick(back_hot[...], heat_recv[...].reshape(SLOTS, 128))

    def sources(z, rb):
        at = pl.ds(pl.multiple_of(z * ROWS + rb * 8, 8), 8)
        source = temp[pl.ds(rb * 32 + z, 8, stride=DEPTH), :] + cells[at, :]
        eighth = 0.125 * source
        for i in range(3):
            moved = eighth * (4.0 * vel[i, z, pl.ds(rb * 8, 8), :])
            thermal[2 * i, z + 1, pl.ds(rb * 8 + PAD, 8), :] = eighth + moved
            thermal[2 * i + 1, z + 1, pl.ds(rb * 8 + PAD, 8), :] = eighth - moved
        cells[at, :] = 0.25 * source

    th_moves = (
        ((4, 4, body), (4, 0, body), (up, gy)),
        ((5, 1, body), (5, 5, body), (down, gy)),
        ((2, planes, high_src), (2, planes, high_dst), (gz, north)),
        ((3, planes, low_src), (3, planes, low_dst), (gz, south)),
    )
    over(face_tile(0, 9), 18, sources)
    th_copies = send_all(thermal, th_moves[:2], th_s, th_r, 0)
    over(side_tile, 4, sources)
    th_copies += send_all(thermal, th_moves[2:], th_s, th_r, 2)
    over(inner_tile, 14, sources)
    for copy in th_copies:
        copy.wait()
    pltpu.make_async_copy(
        ask_send.at[: N_GY - 1], ask_mid.at[: N_GY - 1], all_s.at[0]
    ).wait()
    pltpu.make_async_copy(others, others, all_s.at[3]).wait()
    for n, ref in ((1, row_send), (2, heat_send)):
        done = ref.at[:, pl.ds(0, DEVICES - 1)]
        pltpu.make_async_copy(done, done, all_s.at[n]).wait()


def finish(field, thermal, cells, out_hbm, temp_out_hbm, temp_out, out_sem, temp_sem):
    copies = []
    for i, (lo, hi) in enumerate(((0, 5), (5, 10), (10, 15), (15, 19))):
        copy = pltpu.make_async_copy(field.at[lo:hi], out_hbm.at[lo:hi], out_sem.at[i])
        copy.start()
        copies.append(copy)

    def gather(z, rb):
        place_x = lax.rem(
            (rb * 8 + tile_iota(0)) * 128 + tile_iota(1), jnp.full((8, 128), ACROSS, jnp.int32)
        )
        left, right = place_x == 0, place_x == ACROSS - 1
        total = cells[pl.ds(pl.multiple_of(z * ROWS + rb * 8, 8), 8), :]
        for i in range(6):
            step_x, step_y, step_z = DIRS[i + 1]
            total = total + shifted(
                window(thermal, (i,), z + 1 - step_z, rb), step_x, step_y, left, right
            )
        temp_out[pl.ds(rb * 32 + z, 8, stride=DEPTH), :] = total

    over(lambda j: (lax.rem(j, 4), lax.div(j, 4)), 36, gather, 12)
    copy = pltpu.make_async_copy(temp_out, temp_out_hbm, temp_sem)
    copy.start()
    copy.wait()
    for copy in copies:
        copy.wait()


def fold(x):
    lead = x.shape[:-2]
    n = len(lead)
    x = x.reshape(lead + (DEPTH, ROWS, 128)).transpose(tuple(range(n)) + (n + 1, n, n + 2))
    return x.reshape(lead + (CELL_ROWS, 128))


def unfold(x):
    lead = x.shape[:-2]
    n = len(lead)
    x = x.reshape(lead + (ROWS, DEPTH, 128)).transpose(tuple(range(n)) + (n + 1, n, n + 2))
    return x.reshape(lead + (DEPTH, ROWS * 128))


def per_device(populations, kinds, temperature, lines, wanted, places, hits, beam):
    f32, i32, bf16 = jnp.float32, jnp.int32, jnp.bfloat16
    dma = pltpu.SemaphoreType.DMA
    vmem = pl.BlockSpec(memory_space=pltpu.VMEM)
    whole = pl.BlockSpec(memory_space=pl.ANY)
    operands = (
        fold(populations),
        fold(kinds),
        fold(temperature),
        lines,
        wanted[0].T,
        places,
        hits,
        beam[0],
    )
    field, thermal, cells = pl.pallas_call(
        kernel,
        out_shape=(
            pltpu.VMEM((19, CELL_ROWS, 128), f32),
            pltpu.VMEM((6, DEPTH + 2, PLANE, 128), f32),
            pltpu.VMEM((384, 128), f32),
        ),
        in_specs=[whole] * 8,
        out_specs=[vmem] * 3,
        scratch_shapes=[
            pltpu.VMEM((19, CELL_ROWS, 128), f32),
            pltpu.VMEM((CELL_ROWS, 128), i32),
            pltpu.VMEM((CELL_ROWS, 128), f32),
            pltpu.VMEM((1, NB_DEV), i32),
            pltpu.VMEM((CAP, DEVICES), i32),
            pltpu.VMEM((1, SLOTS), i32),
            pltpu.VMEM((1, RAYS), i32),
            pltpu.VMEM((RAYS, 128), f32),
            pltpu.VMEM((DEPTH + 2, PLANE, 128), i32),
            pltpu.VMEM((19, DEPTH + 2, PLANE, 128), f32),
            pltpu.VMEM((19, DEPTH + 2, PLANE, 128), f32),
            pltpu.VMEM((DEPTH, ROWS, 128), i32),
            pltpu.VMEM((4, DEPTH, ROWS, 128), f32),
            pltpu.VMEM((N_GY, N_GZ, 128), f32),
            pltpu.VMEM((N_GY, N_GZ, 128), f32),
            pltpu.VMEM((N_GY, N_GZ, 128), f32),
            pltpu.VMEM((CAP, DEVICES, 128), f32),
            pltpu.VMEM((CAP, DEVICES, 128), f32),
            pltpu.VMEM((CAP, DEVICES, 128), f32),
            pltpu.VMEM((CAP, DEVICES, 128), f32),
            pltpu.VMEM((SLOTS, SLOTS), bf16),
            pltpu.VMEM((SLOTS, SLOTS), bf16),
            pltpu.VMEM((SLOTS, 384), bf16),
            pltpu.VMEM((CELL_ROWS, SLOTS), bf16),
            pltpu.VMEM((SLOTS, 128), f32),
            pltpu.VMEM((RAYS, 128), f32),
            dma((9,)),
            dma((7,)),
            dma((8,)),
            dma((8,)),
            dma((30,)),
            dma((30,)),
            dma((4,)),
            dma((4,)),
            dma((4,)),
            dma((4,)),
        ],
        compiler_params=pltpu.CompilerParams(
            collective_id=0, has_side_effects=True, vmem_limit_bytes=40 * 2**20
        ),
        cost_estimate=pl.CostEstimate(
            flops=100_000_000, bytes_accessed=7_000_000, transcendentals=40_000
        ),
    )(*[pltpu.with_memory_space_constraint(x, pltpu.HBM) for x in operands])
    lattice, heated = pl.pallas_call(
        finish,
        out_shape=(
            jax.ShapeDtypeStruct((19, CELL_ROWS, 128), f32),
            jax.ShapeDtypeStruct((CELL_ROWS, 128), f32),
        ),
        in_specs=[vmem] * 3,
        out_specs=[whole] * 2,
        scratch_shapes=[pltpu.VMEM((CELL_ROWS, 128), f32), dma((4,)), dma],
        compiler_params=pltpu.CompilerParams(vmem_limit_bytes=40 * 2**20),
        cost_estimate=pl.CostEstimate(
            flops=1_000_000, bytes_accessed=7_000_000, transcendentals=0
        ),
    )(*[pltpu.with_memory_space_constraint(x, pltpu.VMEM) for x in (field, thermal, cells)])
    return unfold(lattice), unfold(heated)


def solution(mesh):
    placed = (
        P(None, "gz", "gy"),
        P("gz", "gy"),
        P("gz", "gy"),
        P(("gz", "gy"), None),
        P(("gz", "gy"), None, None),
        P(("gz", "gy"), None),
        P(("gz", "gy"), None),
        P(("gz", "gy"), None, None),
    )
    return jax.shard_map(
        per_device,
        mesh=mesh,
        in_specs=placed,
        out_specs=(P(None, "gz", "gy"), P("gz", "gy")),
        check_vma=False,
    )
```
